32 devices in a mesh: fsdp: 8 (over z, y), rep: 4 (over x, core).
Axes of the slice: x: 2, y: 2, z: 4, core: 2. Of those that a mesh axis runs over, the one named last changes fastest.
Arguments:
- clips_in: bfloat16 [96, 392, 2048], P(('fsdp', 'rep')), may hold values from -6 to 6
- view_ids: int32 [96], P(('fsdp', 'rep')), may hold values from 0 to 32, as said below
- seg_order: int32 [96, 8], P(('fsdp', 'rep')), may hold values from 0 to 7, each once within a row
- reduce_weight: bfloat16 [2048, 512], P('fsdp'), may hold values from -0.125 to 0.125
- gain1: bfloat16 [512], P('fsdp'), may hold values from 0.25 to 1.75
- shift1: bfloat16 [512], P('fsdp'), may hold values from -3 to 3
- diff_weight: bfloat16 [4608, 512], P('fsdp'), may hold values from -0.09375 to 0.09375
- pooled_weight: bfloat16 [512, 512], P('fsdp'), may hold values from -0.25 to 0.25
- spatial_weight: bfloat16 [4608, 512], P('fsdp'), may hold values from -0.09375 to 0.09375
- gain2: bfloat16 [512], P('fsdp'), may hold values from 0.25 to 1.75
- shift2: bfloat16 [512], P('fsdp'), may hold values from -3 to 3
- expand_weight: bfloat16 [512, 2048], P('fsdp'), may hold values from -0.25 to 0.25
- gain3: bfloat16 [2048], P('fsdp'), may hold values from 0.25 to 1.75
- shift3: bfloat16 [2048], P('fsdp'), may hold values from -3 to 3
- class_weight: bfloat16 [2048, 174], P('fsdp'), may hold values from -0.125 to 0.125
- video_cotangent: float32 [32, 174], P(('fsdp', 'rep')), may hold values from -6 to 6
Outputs:
- video_logits: float32 [32, 174], P(('fsdp', 'rep'))
- clips_grad: bfloat16 [96, 392, 2048], P(('fsdp', 'rep'))
- grad_reduce: float32 [2048, 512], P('fsdp')
- grad_gain1: float32 [512], P('fsdp')
- grad_shift1: float32 [512], P('fsdp')
- grad_diff: float32 [4608, 512], P('fsdp')
- grad_pooled: float32 [512, 512], P('fsdp')
- grad_spatial: float32 [4608, 512], P('fsdp')
- grad_gain2: float32 [512], P('fsdp')
- grad_shift2: float32 [512], P('fsdp')
- grad_expand: float32 [512, 2048], P('fsdp')
- grad_gain3: float32 [2048], P('fsdp')
- grad_shift3: float32 [2048], P('fsdp')
- grad_class: float32 [2048, 174], P('fsdp')
The draws below stay inside these ranges and needn't reach their ends.
Inputs may be any that keep to these rules, and one draw needn't show every extreme that they name: `view_ids`: every video 0 to 31 owns 1 to 3 clip slots, some video exactly 3; the other slots are empty and hold 32. `seg_order`: each row is a permutation of the 8 segments.
All inputs are finite; a program needn't handle non-finite values.
Results may differ from the reference program's by a relative error of at most 0.018.
Values may be sent and summed in bfloat16 or wider, within the bound.
No kernel may reach another device: no remote copies, remote signals or barrier semaphores. Data moves between devices by JAX's collectives and lax.ppermute only.
A program may use at most 256 MiB of HBM per device.

```python
import jax
import jax.numpy as jnp
from jax import lax

D = 2048
MID = 512
CLASSES = 174
SEGS = 8
SIDE = 7
MOST = 3
FRAME_ROWS = 392
CLIPS = 96
VIDEOS = 32


def draw_view_ids(key, part):
    key = jax.random.fold_in(key, 17)
    count_key, order_key, fullest_key = jax.random.split(key, 3)
    counts = jax.random.randint(count_key, (VIDEOS,), 1, MOST + 1).astype(jnp.int32)
    fullest = jax.random.randint(fullest_key, (), 0, VIDEOS)
    counts = jnp.where(jnp.arange(VIDEOS, dtype=jnp.int32) == fullest, MOST, counts).astype(jnp.int32)
    boundaries = jnp.cumsum(counts)
    positions = jnp.arange(CLIPS, dtype=jnp.int32)
    owners = jnp.sum((positions[:, None] >= boundaries[None, :]).astype(jnp.int32), axis=1)
    shuffle = jax.random.permutation(order_key, CLIPS)
    return owners[shuffle].astype(jnp.int32)


def level_of(stream_key, dims, cuts, smallest, high):
    gain, own = 1.0, jax.random.fold_in(stream_key, 6)
    for position, blocks in cuts:
        draws = jnp.exp(jax.random.uniform(jax.random.fold_in(own, position), (blocks,), jnp.float32, smallest / len(cuts), high / len(cuts)))
        gain = gain * jnp.repeat(draws, dims[position] // blocks).reshape([-1 if axis == position else 1 for axis in range(len(dims))])
    return gain


def noise(key, shape, scale, bound, cuts=(), held_as=jnp.bfloat16):
    values = scale * jax.random.normal(key, shape, jnp.float32)
    if cuts:
        values = values * level_of(key, shape, cuts, -0.22, 0.18)
    return jnp.clip(values, -bound, bound).astype(held_as)


def setup_inputs(seed: int = 0) -> dict:
    streams_of = jax.random.split(jax.random.key(seed), 17)
    clips_in = noise(streams_of[0], (CLIPS, FRAME_ROWS, D), 1.0, 6.0, ((0, 32),))
    view_ids = draw_view_ids(jax.random.fold_in(streams_of[16], 71), 0)
    seg_order = jax.vmap(lambda own: jax.random.permutation(own, SEGS))(jax.random.split(streams_of[2], CLIPS)).reshape((CLIPS, SEGS)).astype(jnp.int32)
    reduce_weight = noise(streams_of[3], (D, MID), D ** -0.5, 0.125, ((0, 8),))
    gain1 = jnp.clip(1.0 + 0.15 * jax.random.normal(streams_of[4], (MID,), jnp.float32), 0.25, 1.75).astype(jnp.bfloat16)
    shift1 = noise(streams_of[5], (MID,), 0.5, 3.0, ((0, 8),))
    diff_weight = noise(streams_of[6], (9 * MID, MID), (9 * MID) ** -0.5, 0.09375, ((0, 8),))
    pooled_weight = noise(streams_of[7], (MID, MID), MID ** -0.5, 0.25, ((0, 8),))
    spatial_weight = noise(streams_of[8], (9 * MID, MID), (9 * MID) ** -0.5, 0.09375, ((0, 8),))
    gain2 = jnp.clip(1.0 + 0.15 * jax.random.normal(streams_of[9], (MID,), jnp.float32), 0.25, 1.75).astype(jnp.bfloat16)
    shift2 = noise(streams_of[10], (MID,), 0.5, 3.0, ((0, 8),))
    expand_weight = noise(streams_of[11], (MID, D), MID ** -0.5, 0.25, ((0, 8),))
    gain3 = jnp.clip(1.0 + 0.15 * jax.random.normal(streams_of[12], (D,), jnp.float32), 0.25, 1.75).astype(jnp.bfloat16)
    shift3 = noise(streams_of[13], (D,), 0.5, 3.0, ((0, 8),))
    class_weight = noise(streams_of[14], (D, CLASSES), D ** -0.5, 0.125, ((0, 8),))
    video_cotangent = noise(streams_of[15], (VIDEOS, CLASSES), 1.0, 6.0, ((0, 32),), jnp.float32)
    return dict(clips_in=clips_in, view_ids=view_ids, seg_order=seg_order, reduce_weight=reduce_weight, gain1=gain1, shift1=shift1, diff_weight=diff_weight, pooled_weight=pooled_weight, spatial_weight=spatial_weight, gain2=gain2, shift2=shift2, expand_weight=expand_weight, gain3=gain3, shift3=shift3, class_weight=class_weight, video_cotangent=video_cotangent)


epsilon = 1e-05
clip_block = 16
highest = lax.Precision.HIGHEST

@jax.custom_vjp
def low(v):
    return lax.optimization_barrier(v.astype(jnp.bfloat16)).astype(jnp.float32)

@jax.custom_vjp
def low_back(v):
    return v

def low_keep(v):
    return (low(v), None)

def low_pass(kept, grad):
    return (grad,)

def back_keep(v):
    return (v, None)

def back_low(kept, grad):
    return (low(grad),)
low.defvjp(low_keep, low_pass)
low_back.defvjp(back_keep, back_low)

def patches(field):
    extent = field.shape[1]
    padded = jnp.pad(field, ((0, 0), (1, 1), (1, 1), (0, 0)))
    pieces = [padded[:, row_offset:row_offset + extent, column_offset:column_offset + extent, :] for row_offset in range(3) for column_offset in range(3)]
    joined = jnp.concatenate(pieces, axis=3)
    return joined.reshape(-1, joined.shape[3])

def temporal_mix(order):
    length = order.shape[1]
    stations = jnp.arange(length, dtype=jnp.int32)
    places = (order[:, :, None] == stations[None, None, :]).astype(jnp.float32)
    current = places[:, :-1, :]
    upcoming = places[:, 1:, :]
    return lax.optimization_barrier(jnp.sum(current[:, :, :, None] * (upcoming[:, :, None, :] - current[:, :, None, :]), axis=1))

def statistics(values, alive_rows, population):
    center = lax.optimization_barrier(jnp.sum(alive_rows * values, axis=(0, 1))) / population
    spread = lax.optimization_barrier(jnp.sum(alive_rows * (values - center) * (values - center), axis=(0, 1))) / population
    return (center, lax.rsqrt(spread + epsilon))

def reference(clips_in, view_ids, seg_order, reduce_weight, gain1, shift1, diff_weight, pooled_weight, spatial_weight, gain2, shift2, expand_weight, gain3, shift3, class_weight, video_cotangent):
    blocks = CLIPS // clip_block
    block_rows = clip_block * FRAME_ROWS
    alive_clips = (view_ids < VIDEOS).astype(jnp.float32)
    alive_rows = jnp.repeat(alive_clips.reshape(blocks, clip_block), FRAME_ROWS, axis=1)[:, :, None]
    population = jnp.sum(alive_clips) * FRAME_ROWS
    mixers = temporal_mix(seg_order).reshape(blocks, clip_block, SEGS, SEGS)
    members = (view_ids[:, None] == jnp.arange(VIDEOS, dtype=jnp.int32)[None, :]).astype(jnp.float32)
    counts = lax.optimization_barrier(jnp.sum(members, axis=0))
    params = tuple((parameter.astype(jnp.float32) for parameter in (reduce_weight, gain1, shift1, diff_weight, pooled_weight, spatial_weight, gain2, shift2, expand_weight, gain3, shift3, class_weight)))
    inputs = clips_in.astype(jnp.float32)

    def forward(inputs, params):
        w_reduce, g_one, s_one, w_diff, w_pooled, w_spatial, g_two, s_two, w_expand, g_three, s_three, w_class = params
        in_blocks = inputs.reshape(blocks, block_rows, D)

        def reduce_block(block):
            return low_back(jnp.dot(block, w_reduce, precision=highest))
        first_out = lax.map(jax.checkpoint(reduce_block), in_blocks)
        center_one, scale_one = statistics(first_out, alive_rows, population)

        def middle_block(operands):
            reduced, mixing_table = operands
            hidden_one = jax.nn.silu((reduced - center_one) * scale_one * g_one + s_one)
            hidden_one = hidden_one.reshape(clip_block, SEGS, SIDE * SIDE, MID)
            difference = low(jnp.einsum('cji,cipn->cjpn', mixing_table, hidden_one, precision=highest))
            summary = low(lax.optimization_barrier(jnp.mean(difference, axis=2))).reshape(clip_block * SEGS, MID)
            local_term = jnp.dot(patches(difference.reshape(clip_block * SEGS, SIDE, SIDE, MID)), w_diff, precision=highest)
            global_term = jnp.dot(summary, w_pooled, precision=highest)
            gate_logit = low_back(local_term.reshape(clip_block * SEGS, SIDE * SIDE, MID) + global_term[:, None, :])
            gating = jax.nn.sigmoid(gate_logit).reshape(clip_block, SEGS, SIDE * SIDE, MID)
            boosted = low(hidden_one * (1.0 + gating))
            return low_back(jnp.dot(patches(boosted.reshape(clip_block * SEGS, SIDE, SIDE, MID)), w_spatial, precision=highest))
        second_out = lax.map(jax.checkpoint(middle_block), (first_out, mixers))
        center_two, scale_two = statistics(second_out, alive_rows, population)

        def expand_block(mixed):
            hidden_two = low(jax.nn.silu((mixed - center_two) * scale_two * g_two + s_two))
            return low_back(jnp.dot(hidden_two, w_expand, precision=highest))
        third_out = lax.map(jax.checkpoint(expand_block), second_out)
        center_three, scale_three = statistics(third_out, alive_rows, population)

        def classify_block(operands):
            block, expanded = operands
            outcome = jax.nn.silu((expanded - center_three) * scale_three * g_three + s_three + block)
            pooled = low(lax.optimization_barrier(jnp.mean(outcome.reshape(clip_block, FRAME_ROWS, D), axis=1)))
            return low_back(jnp.dot(pooled, w_class, precision=highest))
        clip_logits = lax.map(jax.checkpoint(classify_block), (in_blocks, third_out)).reshape(CLIPS, CLASSES)
        return jnp.dot(members.T, clip_logits, precision=highest) / counts[:, None]
    video_logits, pullback = jax.vjp(forward, inputs, params)
    input_grad, grads = pullback(video_cotangent)
    return (video_logits, input_grad.astype(jnp.bfloat16), grads[0], grads[1], grads[2], grads[3], grads[4], grads[5], grads[6], grads[7], grads[8], grads[9], grads[10], grads[11])
```

```python
import jax
import jax.numpy as jnp
from jax import lax
from jax.sharding import PartitionSpec as P

D = 2048
MID = 512
SEGS = 8
SIDE = 7
FRAME_ROWS = 392
EVERY = ("fsdp", "rep")

epsilon = 1e-05
highest = lax.Precision.HIGHEST
f32 = jnp.float32
bf16 = jnp.bfloat16


def patches(field):
    extent = field.shape[1]
    padded = jnp.pad(field, ((0, 0), (1, 1), (1, 1), (0, 0)))
    pieces = [
        padded[:, row_offset : row_offset + extent, column_offset : column_offset + extent, :]
        for row_offset in range(3)
        for column_offset in range(3)
    ]
    joined = jnp.concatenate(pieces, axis=3)
    return joined.reshape(-1, joined.shape[3])


def flipped(kernel):
    outputs = kernel.shape[1]
    taps = kernel.reshape(9, -1, outputs)[::-1]
    return jnp.swapaxes(taps, 1, 2).reshape(-1, taps.shape[1])


def temporal_mix(order):
    length = order.shape[1]
    stations = jnp.arange(length, dtype=jnp.int32)
    places = (order[:, :, None] == stations[None, None, :]).astype(f32)
    current = places[:, :-1, :]
    upcoming = places[:, 1:, :]
    return jnp.sum(
        current[:, :, :, None] * (upcoming[:, :, None, :] - current[:, :, None, :]), axis=1
    )


def silu_slope(values):
    sigma_part = jax.nn.sigmoid(values)
    return sigma_part * (1.0 + values * (1.0 - sigma_part))


def swap(array, bit):
    count = lax.axis_size("fsdp") * lax.axis_size("rep")
    return lax.ppermute(array, EVERY, [(place, place ^ bit) for place in range(count)])


def in_order(bit, mine, other, axis):
    first = jnp.where(bit == 0, mine, other)
    second = jnp.where(bit == 0, other, mine)
    return jnp.stack([first, second], axis=axis)


def half(array, bit, axis):
    return lax.dynamic_index_in_dim(array, bit, axis=axis, keepdims=False)


class Block:
    def __init__(self):
        place = lax.axis_index("fsdp") * 4 + lax.axis_index("rep")
        self.core = place & 1
        self.x = (place >> 1) & 1
        self.y = (place >> 2) & 1
        self.z0 = (place >> 3) & 1
        self.z1 = (place >> 4) & 1
        self.z = place >> 3

    def gather(self, quarter):
        rows, lanes = quarter.shape
        one, two, three = (swap(quarter, bit) for bit in (8, 16, 24))
        low = in_order(self.z0, quarter, one, 0)
        high = in_order(self.z0, two, three, 0)
        depth = in_order(self.z1, low, high, 0).reshape(4, rows, lanes)
        plane = in_order(self.y, depth, swap(depth, 4), 1)
        plane = in_order(self.x, plane, swap(plane, 2), 2)
        plane = in_order(self.core, plane, swap(plane, 1), 3)
        return plane.reshape(32 * rows, lanes)

    def reduce(self, partial):
        lanes = partial.shape[1]
        rows = partial.shape[0] // 32
        total = partial.reshape(4, 2, 2, 2, rows, lanes)

        def fold(total, bit, mask, axis):
            sent = half(total, 1 - bit, axis).astype(bf16)
            return half(total, bit, axis).astype(f32) + swap(sent, mask).astype(f32)

        total = fold(total, self.core, 1, 3)
        total = fold(total, self.x, 2, 2)
        total = fold(total, self.y, 4, 1)
        arrived = [
            swap(half(total, self.z ^ hop, 0).astype(bf16), 8 * hop).astype(f32)
            for hop in (1, 2, 3)
        ]
        total = half(total, self.z, 0) + arrived[0] + arrived[1] + arrived[2]
        total = total.astype(bf16)
        total = in_order(self.x, total, swap(total, 2), 0)
        total = in_order(self.core, total, swap(total, 1), 1)
        return total.reshape(4 * rows, lanes).astype(f32)


def to_rows(array):
    rows, lanes = array.shape
    return jnp.swapaxes(array.reshape(rows, lanes // 512, 512), 0, 1).reshape(-1, 512)


def from_rows(array, shards, rows, lanes):
    array = array.reshape(shards, lanes // 512, rows, 512)
    return jnp.swapaxes(array, 1, 2).reshape(shards * rows, lanes)


def split_rows(array, sizes):
    shards = array.shape[0] // sum(sizes)
    array = array.reshape(shards, sum(sizes), array.shape[1])
    pieces, start = [], 0
    for size in sizes:
        pieces.append(array[:, start : start + size].reshape(shards * size, -1))
        start += size
    return pieces


def gather_block(shards):
    (reduce_weight, diff_weight, pooled_weight, spatial_weight, expand_weight, class_weight) = shards
    block = Block()
    which = lax.axis_index("rep")

    def own(weight):
        rows = weight.shape[0] // 4
        return lax.dynamic_slice_in_dim(weight, which * rows, rows, axis=0)

    w_reduce = block.gather(own(reduce_weight))
    middle = jnp.concatenate([own(diff_weight), own(pooled_weight)])
    w_diff, w_pooled = split_rows(block.gather(middle), (144, 16))
    w_spatial = block.gather(own(spatial_weight))
    classes = class_weight.shape[1]
    wide = jnp.pad(own(class_weight), ((0, 0), (0, 512 - classes)))
    last = jnp.concatenate([to_rows(own(expand_weight)), wide])
    w_expand, w_class = split_rows(block.gather(last), (64, 64))
    w_expand = from_rows(w_expand, 32, 16, D)
    w_class = w_class[:, :classes]
    return (w_reduce, w_diff, w_pooled, w_spatial, w_expand, w_class)


def reduce_block(grads):
    grad_reduce, grad_diff, grad_pooled, grad_spatial, grad_expand, grad_class = grads
    block = Block()

    def join(arrays):
        pieces = [array.reshape(32, -1, 512) for array in arrays]
        return jnp.concatenate(pieces, axis=1).reshape(-1, 512)

    classes = grad_class.shape[1]
    wide = jnp.pad(grad_class, ((0, 0), (0, 512 - classes)))
    narrow = jnp.swapaxes(grad_expand.reshape(32, 16, 4, 512), 1, 2).reshape(-1, 512)
    last = block.reduce(join([narrow, wide])).reshape(4, 128, 512)
    out_expand = jnp.swapaxes(last[:, :64].reshape(4, 4, 16, 512), 1, 2).reshape(64, D)
    out_class = last[:, 64:].reshape(256, 512)[:, :classes]
    out_spatial = block.reduce(grad_spatial)
    middle = block.reduce(join([grad_diff, grad_pooled])).reshape(4, 160, 512)
    out_diff = middle[:, :144].reshape(576, 512)
    out_pooled = middle[:, 144:].reshape(64, 512)
    out_reduce = block.reduce(grad_reduce)
    return (out_reduce, out_diff, out_pooled, out_spatial, out_expand, out_class)


def gather_any(shards):
    return tuple(lax.all_gather(shard, "fsdp", axis=0, tiled=True) for shard in shards)


def reduce_any(grads):
    sums = tuple(
        lax.psum_scatter(grad, "fsdp", scatter_dimension=0, tiled=True) for grad in grads
    )
    return lax.psum(sums, "rep")


def exchange(payload):
    return lax.all_to_all(payload, EVERY, 0, 0, tiled=True)


def share(vector):
    count = lax.axis_size("fsdp") * lax.axis_size("rep")
    return exchange(jnp.broadcast_to(vector[None], (count, vector.shape[0])))


def local_moments(values, alive_rows, own_count):
    mean = jnp.sum(alive_rows * values, axis=0) / jnp.maximum(own_count, 1.0)
    deviation = values - mean
    return mean, jnp.sum(alive_rows * deviation * deviation, axis=0)


def joint_moments(means, squares, every_count, weight_sum):
    center = jnp.sum(every_count * means, axis=0) / weight_sum
    offset = means - center
    spread = jnp.sum(squares + every_count * offset * offset, axis=0) / weight_sum
    return center, lax.rsqrt(spread + epsilon)


def norm_input_grad(grad_out, normed, alive_rows, gain, scale, weight_sum, shift_grad, gain_grad):
    return gain * scale * (grad_out - alive_rows * (shift_grad + normed * gain_grad) / weight_sum)


def local(
    clips_in,
    view_ids,
    seg_order,
    reduce_weight,
    gain1,
    shift1,
    diff_weight,
    pooled_weight,
    spatial_weight,
    gain2,
    shift2,
    expand_weight,
    gain3,
    shift3,
    class_weight,
    video_cotangent,
):
    fsdp_count = lax.axis_size("fsdp")
    rep_count = lax.axis_size("rep")
    devices = fsdp_count * rep_count
    clip_count = clips_in.shape[0]
    planes = clip_count * SEGS
    pixels = SIDE * SIDE
    own_videos, classes = video_cotangent.shape
    videos_all = own_videos * devices
    on_block = (fsdp_count, rep_count) == (8, 4)

    alive_clips = (view_ids < videos_all).astype(f32)
    alive_rows = jnp.repeat(alive_clips, FRAME_ROWS)[:, None]
    own_count = jnp.sum(alive_clips) * FRAME_ROWS
    members = (view_ids[:, None] == jnp.arange(videos_all, dtype=jnp.int32)[None, :]).astype(f32)
    mixing_table = temporal_mix(seg_order)

    weights = (reduce_weight, diff_weight, pooled_weight, spatial_weight, expand_weight, class_weight)
    gather = gather_block if on_block else gather_any
    w_reduce, w_diff, w_pooled, w_spatial, w_expand, w_class = gather(weights)

    flat_in = clips_in.reshape(-1, D)
    first_out = jnp.dot(flat_in, w_reduce, preferred_element_type=f32)
    own_mean, own_square = local_moments(first_out, alive_rows, own_count)
    vectors = (gain1, shift1, gain2, shift2, gain3, shift3)
    lengths = [vector.shape[0] for vector in vectors]
    payload = [own_mean, own_square, view_ids.astype(f32), video_cotangent.reshape(-1)]
    payload += [vector.astype(f32) for vector in vectors]
    got = share(jnp.concatenate(payload))
    cuts = []
    start = 0
    for piece in payload:
        cuts.append(got[:, start : start + piece.shape[0]])
        start += piece.shape[0]
    every_view = cuts[2].reshape(-1)
    every_alive = (cuts[2] < videos_all).astype(f32)
    every_count = jnp.sum(every_alive, axis=1, keepdims=True) * FRAME_ROWS
    weight_sum = jnp.sum(every_count)
    every_cotangent = cuts[3].reshape(videos_all, classes)
    g_one, s_one, g_two, s_two, g_three, s_three = (
        piece.reshape(fsdp_count, rep_count, -1)[:, 0].reshape(-1) for piece in cuts[4:]
    )
    counts = jnp.sum(
        (every_view[:, None] == jnp.arange(videos_all, dtype=f32)[None, :]).astype(f32), axis=0
    )
    center_one, scale_one = joint_moments(cuts[0], cuts[1], every_count, weight_sum)

    normed_one = (first_out - center_one) * scale_one
    pre_one = normed_one * g_one + s_one
    hidden_one = jax.nn.silu(pre_one).reshape(clip_count, SEGS, pixels, MID)
    difference = jnp.einsum("cji,cipn->cjpn", mixing_table, hidden_one, precision=highest).astype(bf16)
    summary = jnp.mean(difference.astype(f32), axis=2).astype(bf16).reshape(planes, MID)
    difference_patches = patches(difference.reshape(planes, SIDE, SIDE, MID))
    local_term = jnp.dot(difference_patches, w_diff, preferred_element_type=f32).reshape(
        planes, pixels, MID
    )
    global_term = jnp.dot(summary, w_pooled, preferred_element_type=f32)
    gating = jax.nn.sigmoid(local_term + global_term[:, None, :]).reshape(
        clip_count, SEGS, pixels, MID
    )
    boosted = (hidden_one * (1.0 + gating)).astype(bf16)
    boosted_patches = patches(boosted.reshape(planes, SIDE, SIDE, MID))
    second_out = jnp.dot(boosted_patches, w_spatial, preferred_element_type=f32)
    got = share(jnp.concatenate(local_moments(second_out, alive_rows, own_count)))
    center_two, scale_two = joint_moments(got[:, :MID], got[:, MID:], every_count, weight_sum)

    normed_two = (second_out - center_two) * scale_two
    pre_two = normed_two * g_two + s_two
    hidden_two = jax.nn.silu(pre_two).astype(bf16)
    third_out = jnp.dot(hidden_two, w_expand, preferred_element_type=f32)
    got = share(jnp.concatenate(local_moments(third_out, alive_rows, own_count)))
    center_three, scale_three = joint_moments(got[:, :D], got[:, D:], every_count, weight_sum)

    normed_three = (third_out - center_three) * scale_three
    summed = normed_three * g_three + s_three + flat_in.astype(f32)
    outcome = jax.nn.silu(summed)
    pooled = jnp.mean(outcome.reshape(clip_count, FRAME_ROWS, D), axis=1).astype(bf16)
    clip_logits = jnp.dot(pooled, w_class, preferred_element_type=f32)
    video_sums = jnp.dot(members.T, clip_logits, precision=highest)

    every_share = every_cotangent / counts[:, None]
    logit_grad = jnp.dot(members, every_share, precision=highest).astype(bf16)
    grad_class = jnp.dot(pooled.T, logit_grad, preferred_element_type=f32)
    pooled_grad = jnp.dot(logit_grad, w_class.T, preferred_element_type=f32)
    summed_grad = (
        pooled_grad[:, None, :] / FRAME_ROWS * silu_slope(summed).reshape(clip_count, FRAME_ROWS, D)
    ).reshape(-1, D)

    def norm_sums(grad_out, normed):
        return jnp.concatenate(
            [
                jnp.sum(alive_rows * grad_out, axis=0),
                jnp.sum(alive_rows * grad_out * normed, axis=0),
            ]
        )

    sums = norm_sums(summed_grad, normed_three)
    got = exchange(
        jnp.concatenate(
            [
                jnp.broadcast_to(sums[None], (devices, sums.shape[0])),
                video_sums.reshape(devices, own_videos * classes),
            ],
            axis=1,
        )
    )
    got = jnp.sum(got, axis=0)
    shift_three_grad, gain_three_grad = got[:D], got[D : 2 * D]
    video_total = got[2 * D :].reshape(own_videos, classes)
    place = lax.axis_index("fsdp") * rep_count + lax.axis_index("rep")
    own_counts = lax.dynamic_slice_in_dim(counts, place * own_videos, own_videos)
    video_logits = video_total / own_counts[:, None]

    third_low = norm_input_grad(
        summed_grad, normed_three, alive_rows, g_three, scale_three, weight_sum, shift_three_grad, gain_three_grad
    ).astype(bf16)
    grad_expand = jnp.dot(hidden_two.T, third_low, preferred_element_type=f32)
    pre_two_grad = jnp.dot(third_low, w_expand.T, preferred_element_type=f32) * silu_slope(pre_two)
    got = jnp.sum(share(norm_sums(pre_two_grad, normed_two)), axis=0)
    shift_two_grad, gain_two_grad = got[:MID], got[MID:]
    second_low = norm_input_grad(
        pre_two_grad, normed_two, alive_rows, g_two, scale_two, weight_sum, shift_two_grad, gain_two_grad
    ).astype(bf16)
    grad_spatial = jnp.dot(boosted_patches.T, second_low, preferred_element_type=f32)
    boosted_grad = jnp.dot(
        patches(second_low.reshape(planes, SIDE, SIDE, MID)),
        flipped(w_spatial),
        preferred_element_type=f32,
    ).reshape(clip_count, SEGS, pixels, MID)
    hidden_one_grad = boosted_grad * (1.0 + gating)
    gate_grad = (
        (boosted_grad * hidden_one * gating * (1.0 - gating))
        .astype(bf16)
        .reshape(planes, pixels, MID)
    )
    grad_diff = jnp.dot(
        difference_patches.T, gate_grad.reshape(-1, MID), preferred_element_type=f32
    )
    gate_sums = jnp.sum(gate_grad.astype(f32), axis=1)
    grad_pooled = jnp.dot(summary.astype(f32).T, gate_sums, precision=highest)
    difference_grad = jnp.dot(
        patches(gate_grad.reshape(planes, SIDE, SIDE, MID)),
        flipped(w_diff),
        preferred_element_type=f32,
    ).reshape(planes, pixels, MID)
    summary_grad = jnp.dot(gate_sums, w_pooled.astype(f32).T, precision=highest)
    difference_grad = (difference_grad + summary_grad[:, None, :] / pixels).reshape(
        clip_count, SEGS, pixels, MID
    )
    hidden_one_grad = hidden_one_grad + jnp.einsum(
        "cji,cjpn->cipn", mixing_table, difference_grad, precision=highest
    )
    pre_one_grad = hidden_one_grad.reshape(-1, MID) * silu_slope(pre_one)
    got = jnp.sum(share(norm_sums(pre_one_grad, normed_one)), axis=0)
    shift_one_grad, gain_one_grad = got[:MID], got[MID:]
    first_low = norm_input_grad(
        pre_one_grad, normed_one, alive_rows, g_one, scale_one, weight_sum, shift_one_grad, gain_one_grad
    ).astype(bf16)
    grad_reduce = jnp.dot(flat_in.T, first_low, preferred_element_type=f32)
    input_grad = jnp.dot(first_low, w_reduce.T, preferred_element_type=f32) + summed_grad
    clips_grad = input_grad.astype(bf16).reshape(clip_count, FRAME_ROWS, D)

    reduce = reduce_block if on_block else reduce_any
    reduced = reduce((grad_reduce, grad_diff, grad_pooled, grad_spatial, grad_expand, grad_class))
    shard_index = lax.axis_index("fsdp")

    def own_piece(vector):
        piece_length = vector.shape[0] // fsdp_count
        return lax.dynamic_slice_in_dim(vector, shard_index * piece_length, piece_length)

    return (
        video_logits,
        clips_grad,
        reduced[0],
        own_piece(gain_one_grad),
        own_piece(shift_one_grad),
        reduced[1],
        reduced[2],
        reduced[3],
        own_piece(gain_two_grad),
        own_piece(shift_two_grad),
        reduced[4],
        own_piece(gain_three_grad),
        own_piece(shift_three_grad),
        reduced[5],
    )


def solution(mesh):
    clips, weight, vector = P(EVERY, None, None), P("fsdp", None), P("fsdp")
    rows = P(EVERY, None)
    placed = (
        clips, P(EVERY), rows,
        weight, vector, vector,
        weight, weight, weight, vector, vector,
        weight, vector, vector,
        weight, rows,
    )
    return jax.shard_map(
        local,
        mesh=mesh,
        in_specs=placed,
        out_specs=(
            rows, clips,
            weight, vector, vector,
            weight, weight, weight, vector, vector,
            weight, vector, vector,
            weight,
        ),
        check_vma=False,
    )
```

```python
import jax
import jax.numpy as jnp
from jax import lax
from jax.experimental import pallas as pl
from jax.experimental.pallas import tpu as pltpu
from jax.sharding import PartitionSpec as P

D = 2048
MID = 512
EVERY = ("fsdp", "rep")

epsilon = 1e-05
f32 = jnp.float32
bf16 = jnp.bfloat16

SEGS = 8
SIDE = 7
PIXELS = SIDE * SIDE
FRAME_ROWS = SEGS * PIXELS
WIDE = SIDE + 1
VMEM_LIMIT = 58 * 2**20


class Grid:
    def __init__(self, clips):
        self.clips = clips
        self.planes = clips * SEGS
        self.rows = SIDE * WIDE * self.planes
        self.lead = -(-((WIDE + 1) * self.planes) // 16) * 16
        self.total = self.rows + 2 * self.lead
        self.offsets = [
            (WIDE * dy + dx) * self.planes for dy in (-1, 0, 1) for dx in (-1, 0, 1)
        ]

    @classmethod
    def of(cls, total):
        clips = 1
        while cls(clips).total < total:
            clips += 1
        return cls(clips)

    def tap(self, even, odd, tap, start, count):
        offset = self.offsets[tap]
        if offset % 16 == 0:
            return even[pl.ds(self.lead + start + offset, count), :]
        return odd[pl.ds(self.lead + start + offset - 8, count), :]

    def clear_edges(self, field):
        zeros = jnp.zeros((self.lead, MID), f32)
        field[pl.ds(0, self.lead), :] = zeros
        field[pl.ds(self.lead + self.rows, self.lead), :] = zeros
        field[pl.ds(self.total, 8), :] = zeros[:8]

    def pack(self, field, even, odd):
        step = self.total // 7

        @pl.loop(0, 7)
        def _(i):
            start = pl.multiple_of(i * step, 16)
            even[pl.ds(start, step), :] = field[pl.ds(start, step), :].astype(bf16)
            odd[pl.ds(start, step), :] = field[pl.ds(start + 8, step), :].astype(bf16)


def sigmoid(values):
    return 0.5 * jnp.tanh(0.5 * values) + 0.5


def quarters(ref, rows=slice(None)):
    return jnp.concatenate([ref[block, rows, :] for block in range(4)], axis=1)


def put_quarters(ref, rows, value):
    for block in range(4):
        ref[block, rows, :] = value[:, block * 128 : (block + 1) * 128]


def clip_pixel(clip, pixel):
    return pl.ds(clip * FRAME_ROWS + pixel, SEGS, stride=PIXELS)


def send_out(payload, low, high):
    count, _, lanes = payload.shape
    for row in range(4):
        for at, vector in ((row, low), (row + 4, high)):
            payload[:, at, :] = jnp.broadcast_to(
                vector[:, row * lanes : (row + 1) * lanes], (count, lanes)
            )


def received(got, at):
    return jnp.concatenate([got[:, row, :] for row in range(at, at + 4)], axis=1)


def joint_moments(got, counts):
    count = counts[...]
    population = jnp.sum(count, axis=0, keepdims=True)
    means, squares = received(got, 0), received(got, 4)
    center = jnp.sum(count * means, axis=0, keepdims=True) / population
    offset = means - center
    spread = jnp.sum(squares + count * offset * offset, axis=0, keepdims=True) / population
    return center, lax.rsqrt(spread + epsilon)


def own_moments(alive, means, squares):
    clips = len(means)
    alive_sum = sum(alive[clip] for clip in range(clips))
    mean = sum(alive[clip] * means[clip] for clip in range(clips)) / jnp.maximum(alive_sum, 1.0)
    square = 0.0
    for clip in range(clips):
        offset = means[clip] - mean
        square = square + alive[clip] * (squares[clip] + FRAME_ROWS * offset * offset)
    return mean, square


def clip_moments(values):
    mean = jnp.sum(values, axis=0, keepdims=True) * (1.0 / FRAME_ROWS)
    offset = values - mean
    return mean, jnp.sum(offset * offset, axis=0, keepdims=True)


def joint_sums(got, counts):
    population = jnp.sum(counts[...], axis=0, keepdims=True)
    total = jnp.sum(got[...], axis=0)
    low = jnp.concatenate([total[row : row + 1] for row in range(4)], axis=1)
    high = jnp.concatenate([total[row : row + 1] for row in range(4, 8)], axis=1)
    return low, high, low / population, high / population


def contract_rows(left, right):
    return lax.dot_general(left, right, (((0,), (0,)), ((), ())), preferred_element_type=f32)


def contract_lanes(left, right):
    return lax.dot_general(left, right, (((1,), (1,)), ((), ())), preferred_element_type=f32)


def dot(left, right):
    return jnp.dot(left, right, preferred_element_type=f32)


def first_kernel(alive, clips_in, w_reduce, first, payload, means, squares):
    clip = pl.program_id(0)
    first[0] = dot(clips_in[0], w_reduce[...])
    mean, square = clip_moments(first[0])
    means[clip] = mean
    squares[clip] = square

    @pl.when(clip == pl.num_programs(0) - 1)
    def _():
        count = means.shape[0]
        mean, square = own_moments(
            alive, [means[i] for i in range(count)], [squares[i] for i in range(count)]
        )
        send_out(payload, mean, square)


def gate_kernel(
    got, counts, first, gain, shift, following, later, w_diff, w_pooled,
    norm, hidden, gating, diff_even, diff_odd, boost_even, boost_odd, summary,
    natural, field, weight, sem,
):
    grid = Grid(first.shape[0])
    fetch = pltpu.make_async_copy(w_diff, weight, sem)
    fetch.start()
    center, scale = joint_moments(got, counts)
    norm[0:1] = center
    norm[1:2] = scale
    ratio = scale * gain[...]
    for clip in range(grid.clips):

        @pl.loop(0, SIDE)
        def _(part):
            rows = pl.ds(pl.multiple_of(part * 56, 8), 56)
            pre = (first[clip, rows, :] - center) * ratio + shift[...]
            value = pre * sigmoid(pre)
            put_quarters(natural, pl.ds(pl.multiple_of(clip * FRAME_ROWS + part * 56, 8), 56), value)

    grid.clear_edges(field)
    zeros = jnp.zeros((grid.planes, MID), f32)

    def spread_row(y, totals):
        base = pl.multiple_of(y * (WIDE * grid.planes), 8)
        totals = list(totals)
        for x in range(SIDE):
            for clip in range(grid.clips):
                at = base + x * grid.planes + clip * SEGS
                own = quarters(natural, clip_pixel(clip, y * SIDE + x))
                index = following[pl.ds(clip * SEGS, SEGS), :]
                after = jnp.concatenate(
                    [
                        jnp.take_along_axis(own[:, b * 128 : (b + 1) * 128], index, axis=0)
                        for b in range(4)
                    ],
                    axis=1,
                )
                step = (after - own) * later[pl.ds(clip * SEGS, SEGS), 0:1]
                step = step.astype(bf16).astype(f32)
                hidden[pl.ds(at, SEGS), :] = own
                field[pl.ds(grid.lead + at, SEGS), :] = step
                totals[clip] = totals[clip] + step
        edge = base + SIDE * grid.planes
        hidden[pl.ds(edge, grid.planes), :] = zeros
        field[pl.ds(grid.lead + edge, grid.planes), :] = zeros
        return tuple(totals)

    totals = lax.fori_loop(0, SIDE, spread_row, (zeros[:SEGS],) * grid.clips)
    mean = (jnp.concatenate(totals, axis=0) * (1.0 / PIXELS)).astype(bf16)
    summary[...] = mean.astype(f32)
    pooled_term = dot(mean, w_pooled[...])
    grid.pack(field, diff_even, diff_odd)
    fetch.wait()
    part = grid.rows // 2
    for start in (0, part):
        total = None
        for tap in range(9):
            term = dot(grid.tap(diff_even, diff_odd, tap, start, part), weight[pl.ds(tap * MID, MID), :])
            total = term if total is None else total + term
        gating[pl.ds(start, part), :] = total

    def boost(pixel):
        rows = pl.ds(pl.multiple_of(pixel * grid.planes, 8), grid.planes)
        gate = sigmoid(gating[rows, :] + pooled_term)
        gating[rows, :] = gate
        value = hidden[rows, :] * (1.0 + gate)
        field[pl.ds(pl.multiple_of(grid.lead + pixel * grid.planes, 8), grid.planes), :] = value

    pl.loop(0, SIDE * WIDE)(boost)
    grid.pack(field, boost_even, boost_odd)


def spatial_kernel(
    alive, boost_even, boost_odd, w_spatial, second, payload, natural, field
):
    grid = Grid(second.shape[0])
    part = grid.rows // 2
    for start in (0, part):
        total = None
        for tap in range(9):
            term = dot(grid.tap(boost_even, boost_odd, tap, start, part), w_spatial[pl.ds(tap * MID, MID), :])
            total = term if total is None else total + term
        field[pl.ds(start, part), :] = total
    to_natural(grid, lambda at, clip: field[pl.ds(at, SEGS), :], natural)
    means, squares = [], []
    for clip in range(grid.clips):
        second[clip] = quarters(natural, pl.ds(clip * FRAME_ROWS, FRAME_ROWS))
        mean, square = clip_moments(second[clip])
        means.append(mean)
        squares.append(square)
    mean, square = own_moments(alive, means, squares)
    send_out(payload, mean, square)


def to_natural(grid, tile, natural):
    @pl.loop(0, SIDE)
    def _(y):
        for x in range(SIDE):
            for clip in range(grid.clips):
                at = pl.multiple_of(y * (WIDE * grid.planes), 8) + x * grid.planes + clip * SEGS
                put_quarters(natural, clip_pixel(clip, y * SIDE + x), tile(at, clip))


def expand_kernel(
    alive, got, counts, second, gain, shift, w_expand, norm, hidden, third, payload, means, squares
):
    clip = pl.program_id(0)
    center, scale = joint_moments(got, counts)

    @pl.when(clip == 0)
    def _():
        norm[0:1] = center
        norm[1:2] = scale

    ratio = scale * gain[...]
    pre = (second[0] - center) * ratio + shift[...]
    hidden[0] = (pre * sigmoid(pre)).astype(bf16)
    third[0] = dot(hidden[0], w_expand[...])
    mean, square = clip_moments(third[0])
    means[clip] = mean
    squares[clip] = square

    @pl.when(clip == pl.num_programs(0) - 1)
    def _():
        count = means.shape[0]
        mean, square = own_moments(
            alive, [means[i] for i in range(count)], [squares[i] for i in range(count)]
        )
        send_out(payload, mean, square)


def outcome_kernel(
    alive, got, counts, third, clips_in, gain, shift, logit_grad, w_class, members,
    norm, normed, summed_grad, payload, video_sums, grad_class,
    pooled_grad, sums, pooled, moments,
):
    clip = pl.program_id(0)

    @pl.when(clip == 0)
    def _():
        center, scale = joint_moments(got, counts)
        norm[0:1] = center
        norm[1:2] = scale
        moments[0:1] = center
        moments[1:2] = scale
        pooled_grad[...] = contract_lanes(logit_grad[...], w_class[...]) * (1.0 / FRAME_ROWS)
        sums[...] = jnp.zeros_like(sums)
        pooled[...] = jnp.zeros_like(pooled)

    weight = alive[clip]
    for lane in range(0, D, 512):
        lanes = pl.ds(lane, 512)
        center, scale = moments[0:1, lanes], moments[1:2, lanes]
        g, s = gain[:, lanes], shift[:, lanes]
        slope_grad = pooled_grad[pl.ds(clip, 1), lanes]

        def piece(start, count, carry):
            rows = pl.ds(start, count)
            value = (third[0, rows, lanes] - center) * scale
            total = value * g + s + clips_in[0, rows, lanes].astype(f32)
            sigma = sigmoid(total)
            out = total * sigma
            grad = slope_grad * (sigma + out * (1.0 - sigma))
            normed[0, rows, lanes] = value.astype(bf16)
            summed_grad[0, rows, lanes] = grad.astype(bf16)
            eights = lambda v: jnp.sum(v.reshape(count // 8, 8, 512), axis=0)
            return (
                carry[0] + eights(grad),
                carry[1] + eights(grad * value),
                carry[2] + eights(out),
            )

        zero = jnp.zeros((8, 512), f32)
        carry = lax.fori_loop(
            0, FRAME_ROWS // 16, lambda i, c: piece(pl.multiple_of(i * 16, 16), 16, c), (zero,) * 3
        )
        tail = FRAME_ROWS - FRAME_ROWS % 16
        if tail < FRAME_ROWS:
            carry = piece(tail, FRAME_ROWS - tail, carry)
        low, high, mean = (jnp.sum(v, axis=0, keepdims=True) for v in carry)
        sums[0:1, lanes] = sums[0:1, lanes] + weight * low
        sums[1:2, lanes] = sums[1:2, lanes] + weight * high
        pooled[pl.ds(clip, 1), lanes] = mean * (1.0 / FRAME_ROWS)

    @pl.when(clip == pl.num_programs(0) - 1)
    def _():
        send_out(payload, sums[0:1], sums[1:2])
        rounded = pooled[...].astype(bf16)
        logits = dot(rounded, w_class[...])
        total = 0.0
        for i in range(clips_of(members)):
            total = total + members[:, i : i + 1] * logits[i : i + 1]
        video_sums[...] = total
        grad_class[...] = contract_rows(rounded, logit_grad[...]).astype(grad_class.dtype)


def clips_of(members):
    return members.shape[1]


def third_kernel(
    alive, got, counts, normed, summed_grad, gain, norm_three, hidden, w_expand, second, norm_two, gain_two, shift_two,
    grad_expand, pre_grad, payload, grads, total, sums, low, columns,
):
    clip = pl.program_id(0)

    @pl.when(clip == 0)
    def _():
        total[...] = jnp.zeros_like(total)
        columns[...] = jnp.zeros_like(columns)
        sums[...] = jnp.zeros_like(sums)
        shift_grad, gain_grad, shift_share, gain_share = joint_sums(got, counts)
        grads[0:1] = shift_grad
        grads[1:2] = gain_grad
        columns[1:2] = shift_share
        columns[2:3] = gain_share

    weight = alive[clip]
    ratio = gain[...] * norm_three[1:2]
    for lane in range(0, D, 512):
        lanes = pl.ds(lane, 512)
        shift_share, gain_share = columns[1:2, lanes] * weight, columns[2:3, lanes] * weight
        r = ratio[:, lane : lane + 512]

        def piece(start, count, carry):
            rows = pl.ds(start, count)
            value = summed_grad[0, rows, lanes].astype(f32) - (
                shift_share + normed[0, rows, lanes].astype(f32) * gain_share
            )
            value = (r * value).astype(bf16)
            low[rows, lanes] = value
            return carry + jnp.sum(value.astype(f32).reshape(count // 8, 8, 512), axis=0)

        carry = lax.fori_loop(
            0,
            FRAME_ROWS // 16,
            lambda i, c: piece(pl.multiple_of(i * 16, 16), 16, c),
            jnp.zeros((8, 512), f32),
        )
        tail = FRAME_ROWS - FRAME_ROWS % 16
        if tail < FRAME_ROWS:
            carry = piece(tail, FRAME_ROWS - tail, carry)
        columns[0:1, lanes] = columns[0:1, lanes] + jnp.sum(carry, axis=0, keepdims=True)
    grad_out = low[pl.ds(0, FRAME_ROWS), :]
    total[...] = total[...] + contract_rows(hidden[0], grad_out)
    back = contract_lanes(grad_out, w_expand[...])
    value = (second[0] - norm_two[0:1]) * norm_two[1:2]
    pre = value * gain_two[...] + shift_two[...]
    sigma = sigmoid(pre)
    grad = back * (sigma * (1.0 + pre * (1.0 - sigma)))
    pre_grad[0] = grad
    sums[0:1] = sums[0:1] + weight * jnp.sum(grad, axis=0, keepdims=True)
    sums[1:2] = sums[1:2] + weight * jnp.sum(grad * value, axis=0, keepdims=True)

    @pl.when(clip == pl.num_programs(0) - 1)
    def _():
        send_out(payload, sums[0:1], sums[1:2])
        mean = usual_silu(shift_two[...], gain_two[...])
        offset = outer(mean, columns[0:1])
        grad_expand[...] = (total[...] - offset).astype(grad_expand.dtype)


def usual_silu(shift, gain):
    silu = lambda v: v * sigmoid(v)
    wide = 3.0**0.5 * gain
    return (2.0 / 3.0) * silu(shift) + (silu(shift + wide) + silu(shift - wide)) * (1.0 / 6.0)


def outer(column, row):
    return jnp.swapaxes(jnp.broadcast_to(column, (8, column.shape[1])), 0, 1)[:, 0:1] * row


def to_grid(grid, natural, put):
    @pl.loop(0, SIDE)
    def _(y):
        base = pl.multiple_of(y * (WIDE * grid.planes), 8)
        for x in range(SIDE):
            for clip in range(grid.clips):
                put(base + x * grid.planes + clip * SEGS, clip, quarters(natural, clip_pixel(clip, y * SIDE + x)))
        put(base + SIDE * grid.planes, None, jnp.zeros((grid.planes, MID), f32))


def second_kernel(
    alive, got, counts, pre_grad, second, norm_two, gain_two, gain_one, shift_one, boost_even, boost_odd,
    grads, low_even, low_odd, grad_spatial, natural, field,
):
    grid = Grid(pre_grad.shape[0])
    shift_grad, gain_grad, shift_share, gain_share = joint_sums(got, counts)
    grads[0:1] = shift_grad
    grads[1:2] = gain_grad
    center, scale = norm_two[0:1], norm_two[1:2]
    ratio = gain_two[...] * scale
    columns = jnp.zeros((8, MID), f32)
    for clip in range(grid.clips):
        weight = alive[clip]

        def piece(part, columns):
            rows = pl.ds(pl.multiple_of(part * 56, 8), 56)
            value = (second[clip, rows, :] - center) * scale
            grad = ratio * (pre_grad[clip, rows, :] - weight * (shift_share + value * gain_share))
            grad = grad.astype(bf16).astype(f32)
            put_quarters(natural, pl.ds(pl.multiple_of(clip * FRAME_ROWS + part * 56, 8), 56), grad)
            return columns + jnp.sum(grad.reshape(7, 8, MID), axis=0)

        columns = lax.fori_loop(0, SIDE, piece, columns)
    columns = jnp.sum(columns, axis=0, keepdims=True)
    grid.clear_edges(field)

    def put(at, clip, value):
        field[pl.ds(grid.lead + at, value.shape[0]), :] = value

    to_grid(grid, natural, put)
    grid.pack(field, low_even, low_odd)
    offset = outer(1.5 * usual_silu(shift_one[...], gain_one[...]), columns)
    grad_out = low_even[pl.ds(grid.lead, grid.rows), :]
    for tap in range(9):
        term = contract_rows(grid.tap(boost_even, boost_odd, tap, 0, grid.rows), grad_out)
        grad_spatial[pl.ds(tap * MID, MID), :] = (term - offset).astype(grad_spatial.dtype)


def boost_back_kernel(
    low_even, low_odd, w_spatial, hidden, gating, summary, w_pooled,
    hidden_grad, gate_even, gate_odd, grad_pooled, summary_grad, field,
):
    grid = Grid(hidden.shape[0] // (SIDE * WIDE * SEGS))
    part = grid.rows // 2
    for start in (0, part):
        total = None
        for tap in range(9):
            term = contract_lanes(
                grid.tap(low_even, low_odd, 8 - tap, start, part), w_spatial[pl.ds(tap * MID, MID), :]
            )
            total = term if total is None else total + term
        hidden_grad[pl.ds(start, part), :] = total
    grid.clear_edges(field)

    def piece(pixel, total):
        rows = pl.ds(pl.multiple_of(pixel * grid.planes, 8), grid.planes)
        grad, gate = hidden_grad[rows, :], gating[rows, :]
        hidden_grad[rows, :] = grad * (1.0 + gate)
        gate_grad = (grad * hidden[rows, :] * gate * (1.0 - gate)).astype(bf16).astype(f32)
        field[pl.ds(pl.multiple_of(grid.lead + pixel * grid.planes, 8), grid.planes), :] = gate_grad
        return total + gate_grad

    gate_sums = lax.fori_loop(0, SIDE * WIDE, piece, jnp.zeros((grid.planes, MID), f32))
    grid.pack(field, gate_even, gate_odd)
    high = gate_sums.astype(bf16)
    low = (gate_sums - high.astype(f32)).astype(bf16)
    mean = summary[...].astype(bf16)
    grad_pooled[...] = (contract_rows(mean, high) + contract_rows(mean, low)).astype(grad_pooled.dtype)
    back = contract_lanes(high, w_pooled[...]) + contract_lanes(low, w_pooled[...])
    summary_grad[...] = back * (1.0 / PIXELS)


def diff_kernel(diff_even, diff_odd, gate_even, grad_diff):
    grid = Grid.of(gate_even.shape[0])
    grad_out = gate_even[pl.ds(grid.lead, grid.rows), :]
    for tap in range(9):
        term = contract_rows(grid.tap(diff_even, diff_odd, tap, 0, grid.rows), grad_out)
        grad_diff[pl.ds(tap * MID, MID), :] = term.astype(grad_diff.dtype)


def diff_back_kernel(
    alive, gate_even, gate_odd, w_diff, summary_grad, hidden_grad, first, norm_one, gain, shift, before, earlier, later,
    pre_grad, payload, natural, field,
):
    grid = Grid(first.shape[0])
    part = grid.rows // 2
    for start in (0, part):
        total = None
        for tap in range(9):
            term = contract_lanes(
                grid.tap(gate_even, gate_odd, 8 - tap, start, part), w_diff[pl.ds(tap * MID, MID), :]
            )
            total = term if total is None else total + term
        field[pl.ds(start, part), :] = total

    def tile(at, clip):
        planes = pl.ds(clip * SEGS, SEGS)
        grad = field[pl.ds(at, SEGS), :] + summary_grad[planes, :]
        index = before[planes, :]
        back = jnp.concatenate(
            [
                jnp.take_along_axis(grad[:, b * 128 : (b + 1) * 128], index, axis=0)
                for b in range(4)
            ],
            axis=1,
        )
        own = hidden_grad[pl.ds(at, SEGS), :]
        return own + back * earlier[planes, 0:1] - grad * later[planes, 0:1]

    to_natural(grid, tile, natural)
    center, scale = norm_one[0:1], norm_one[1:2]
    low = jnp.zeros((8, MID), f32)
    high = jnp.zeros((8, MID), f32)
    for clip in range(grid.clips):
        weight = alive[clip]

        def piece(step, carry):
            rows = pl.ds(pl.multiple_of(step * 56, 8), 56)
            value = (first[clip, rows, :] - center) * scale
            pre = value * gain[...] + shift[...]
            sigma = sigmoid(pre)
            grad = quarters(natural, pl.ds(pl.multiple_of(clip * FRAME_ROWS + step * 56, 8), 56))
            grad = grad * (sigma * (1.0 + pre * (1.0 - sigma)))
            pre_grad[clip, rows, :] = grad
            eights = lambda v: jnp.sum(v.reshape(7, 8, MID), axis=0) * weight
            return carry[0] + eights(grad), carry[1] + eights(grad * value)

        low, high = lax.fori_loop(0, SIDE, piece, (low, high))
    send_out(payload, jnp.sum(low, axis=0, keepdims=True), jnp.sum(high, axis=0, keepdims=True))


def reduce_kernel(
    alive, got, counts, pre_grad, first, norm_one, gain, clips_in, grads, low, grad_reduce, total
):
    clip = pl.program_id(0)
    shift_grad, gain_grad, shift_share, gain_share = joint_sums(got, counts)

    @pl.when(clip == 0)
    def _():
        total[...] = jnp.zeros_like(total)
        grads[0:1] = shift_grad
        grads[1:2] = gain_grad

    center, scale = norm_one[0:1], norm_one[1:2]
    value = (first[0] - center) * scale
    grad = pre_grad[0] - alive[clip] * (shift_share + value * gain_share)
    low[0] = (gain[...] * scale * grad).astype(bf16)
    total[...] = total[...] + contract_rows(clips_in[0], low[0])

    @pl.when(clip == pl.num_programs(0) - 1)
    def _():
        grad_reduce[...] = total[...].astype(grad_reduce.dtype)


def input_kernel(low, w_reduce, summed_grad, clips_grad):
    back = contract_lanes(low[0], w_reduce[...])
    clips_grad[0] = (back + summed_grad[0].astype(f32)).astype(bf16)


def swap(array, bit):
    count = lax.axis_size("fsdp") * lax.axis_size("rep")
    return lax.ppermute(array, EVERY, [(place, place ^ bit) for place in range(count)])


def in_order(bit, mine, other, axis):
    first = jnp.where(bit == 0, mine, other)
    second = jnp.where(bit == 0, other, mine)
    return jnp.stack([first, second], axis=axis)


def half(array, bit, axis):
    return lax.dynamic_index_in_dim(array, bit, axis=axis, keepdims=False)


class Block:
    def __init__(self):
        self.which = lax.axis_index("rep")
        place = lax.axis_index("fsdp") * 4 + self.which
        self.core = place & 1
        self.x = (place >> 1) & 1
        self.y = (place >> 2) & 1
        self.z0 = (place >> 3) & 1
        self.z1 = (place >> 4) & 1
        self.z = place >> 3

    def own(self, weight):
        rows = weight.shape[0] // 4
        return lax.dynamic_slice_in_dim(weight, self.which * rows, rows, axis=0)

    def gather(self, quarter):
        rows, lanes = quarter.shape
        one, two, three = (swap(quarter, bit) for bit in (8, 16, 24))
        low = in_order(self.z0, quarter, one, 0)
        high = in_order(self.z0, two, three, 0)
        depth = in_order(self.z1, low, high, 0).reshape(4, rows, lanes)
        plane = in_order(self.y, depth, swap(depth, 4), 1)
        plane = in_order(self.x, plane, swap(plane, 2), 2)
        plane = in_order(self.core, plane, swap(plane, 1), 3)
        return plane.reshape(32, rows, lanes)

    def reduce(self, partial):
        _, rows, lanes = partial.shape
        total = partial.reshape(4, 2, 2, 2, rows, lanes)

        def fold(total, bit, mask, axis):
            there = swap(half(total, 1 - bit, axis), mask)
            return (half(total, bit, axis).astype(f32) + there.astype(f32)).astype(bf16)

        total = fold(total, self.core, 1, 3)
        total = fold(total, self.x, 2, 2)
        total = fold(total, self.y, 4, 1)
        arrived = [swap(half(total, self.z ^ hop, 0), 8 * hop) for hop in (1, 2, 3)]
        total = half(total, self.z, 0).astype(f32)
        for there in arrived:
            total = total + there.astype(f32)
        return total

    def spread(self, total):
        rows, lanes = total.shape
        total = total.astype(bf16)
        total = in_order(self.x, total, swap(total, 2), 0)
        total = in_order(self.core, total, swap(total, 1), 1)
        return total.reshape(4, rows, lanes).astype(f32)


def gather_block(reduce_weight, diff_weight, pooled_weight, spatial_weight, expand_weight, class_weight):
    block = Block()
    w_reduce = block.gather(block.own(reduce_weight)).reshape(-1, MID)
    middle = block.gather(jnp.concatenate([block.own(diff_weight), block.own(pooled_weight)]))
    w_diff = middle[:, :144].reshape(-1, MID)
    w_pooled = middle[:, 144:].reshape(-1, MID)
    w_spatial = block.gather(block.own(spatial_weight)).reshape(-1, MID)
    expand = block.own(expand_weight)
    wide = block.own(pad_classes(class_weight))
    last = block.gather(
        jnp.concatenate(
            [expand[:, 512 * i : 512 * (i + 1)] for i in range(4)]
            + [jnp.concatenate([wide[:32], wide[32:]], axis=1)]
        )
    )
    w_expand = jnp.concatenate([last[:, 16 * i : 16 * (i + 1)] for i in range(4)], axis=2)
    w_class = jnp.concatenate([last[:, 64:, :256], last[:, 64:, 256:]], axis=1)
    return w_reduce, w_diff, w_pooled, w_spatial, w_expand.reshape(-1, D), w_class.reshape(D, 256)


def pad_classes(array):
    return jnp.pad(array, ((0, 0), (0, 256 - array.shape[1])))


def reduce_block(grad_reduce, grad_diff, grad_pooled, grad_spatial, grad_expand, grad_class, video_sums):
    block = Block()
    parts = lambda array: array.reshape(32, -1, array.shape[-1])
    expand = parts(grad_expand)
    wide = parts(grad_class)
    last = jnp.concatenate(
        [expand[:, :, 512 * i : 512 * (i + 1)] for i in range(4)]
        + [
            jnp.concatenate([wide[:, :32], wide[:, 32:]], axis=2),
            jnp.pad(video_sums.astype(bf16)[:, None, :], ((0, 0), (0, 15), (0, 256))),
        ],
        axis=1,
    )
    last = block.reduce(last)
    video_total = last[96:97, :256]
    last = block.spread(last[:96])
    out_expand = jnp.concatenate([last[:, 16 * i : 16 * (i + 1)] for i in range(4)], axis=2)
    out_class = jnp.concatenate([last[:, 64:, :256], last[:, 64:, 256:]], axis=1)
    out_spatial = block.spread(block.reduce(parts(grad_spatial)))
    middle = jnp.concatenate([parts(grad_diff), parts(grad_pooled)], axis=1)
    middle = block.spread(block.reduce(middle))
    out_reduce = block.spread(block.reduce(parts(grad_reduce)))
    flat = lambda array: array.reshape(-1, array.shape[-1])
    return (
        flat(out_reduce), flat(middle[:, :144]), flat(middle[:, 144:]), flat(out_spatial),
        flat(out_expand), flat(out_class), video_total,
    )


def gather_any(*shards):
    gathered = [lax.all_gather(shard, "fsdp", axis=0, tiled=True) for shard in shards]
    gathered[5] = pad_classes(gathered[5])
    return gathered


def reduce_any(*grads):
    sums = tuple(
        lax.psum_scatter(grad.astype(f32), "fsdp", scatter_dimension=0, tiled=True)
        for grad in grads[:6]
    )
    videos = lax.psum_scatter(grads[6], EVERY, scatter_dimension=0, tiled=True)
    return *lax.psum(sums, "rep"), videos


def exchange(payload):
    return lax.all_to_all(payload, EVERY, 0, 0, tiled=True)


SCALARS = pl.BlockSpec(memory_space=pltpu.SMEM)
WHOLE = pl.BlockSpec(memory_space=pltpu.VMEM)
ANY = pl.BlockSpec(memory_space=pl.ANY)


def each_clip(shape):
    return pl.BlockSpec((1, *shape[1:]), lambda clip: (clip, 0, 0))


def shaped(shape, dtype=f32):
    return jax.ShapeDtypeStruct(tuple(shape), dtype)


def call(kernel, name, ins, outs, scratch=(), clips=None):
    return pl.pallas_call(
        kernel,
        out_shape=[shape for shape, _ in outs],
        grid=(clips,) if clips else (),
        in_specs=[spec for _, spec in ins],
        out_specs=[spec for _, spec in outs],
        scratch_shapes=list(scratch),
        compiler_params=pltpu.CompilerParams(vmem_limit_bytes=VMEM_LIMIT),
        name=name,
    )(*[array for array, _ in ins])


def local(
    clips_in,
    view_ids,
    seg_order,
    reduce_weight,
    gain1,
    shift1,
    diff_weight,
    pooled_weight,
    spatial_weight,
    gain2,
    shift2,
    expand_weight,
    gain3,
    shift3,
    class_weight,
    video_cotangent,
):
    fsdp_count = lax.axis_size("fsdp")
    rep_count = lax.axis_size("rep")
    devices = fsdp_count * rep_count
    clips = clips_in.shape[0]
    own_videos, classes = video_cotangent.shape
    videos_all = own_videos * devices
    on_block = (fsdp_count, rep_count) == (8, 4)
    grid = Grid(clips)
    planes = grid.planes

    vectors = (gain1, shift1, gain2, shift2, gain3, shift3)
    early = [view_ids.astype(f32), video_cotangent.reshape(-1)]
    early += [vector.astype(f32) for vector in vectors]
    early = jnp.concatenate(early)
    room = -(-early.shape[0] // 1024) * 1024
    early = jnp.pad(early, (0, room - early.shape[0])).reshape(1, 8, room // 8)
    got = exchange(jnp.broadcast_to(early, (devices, 8, room // 8))).reshape(devices, room)
    every_view = got[:, :clips]
    every_alive = (every_view < videos_all).astype(f32)
    counts = jnp.sum(every_alive, axis=1, keepdims=True) * FRAME_ROWS
    start = clips + own_videos * classes
    every_cotangent = got[:, clips:start].reshape(videos_all, classes)
    params = []
    for vector in vectors:
        params.append(got[::rep_count, start : start + vector.shape[0]].reshape(1, -1))
        start += vector.shape[0]
    g_one, s_one, g_two, s_two, g_three, s_three = params
    video_list = jnp.arange(videos_all, dtype=jnp.int32)
    video_count = jnp.sum(
        (every_view.reshape(1, -1) == video_list.astype(f32)[:, None]).astype(f32), axis=1
    )
    members = (video_list[:, None] == view_ids[None, :]).astype(f32)
    alive = (view_ids < videos_all).astype(f32)
    every_share = every_cotangent / video_count[:, None]
    logit_grad = jnp.sum(members[:, :, None] * every_share[:, None, :], axis=0)
    logit_grad = jnp.pad(logit_grad.astype(bf16), ((0, 8 - clips), (0, 256 - classes)))

    stations = jnp.arange(SEGS, dtype=jnp.int32)
    places = (seg_order[:, :, None] == stations).astype(jnp.int32)
    place = jnp.sum(places * stations[None, :, None], axis=1)
    is_last, is_first = place == SEGS - 1, place == 0
    at = lambda wanted: jnp.sum(
        (jnp.clip(wanted, 0, SEGS - 1)[:, :, None] == stations).astype(jnp.int32)
        * seg_order[:, None, :],
        axis=2,
    )
    lanes = lambda array: jnp.broadcast_to(array.reshape(planes, 1), (planes, 128))
    following = lanes(at(place + 1))
    before = lanes(at(place - 1))
    later = lanes(1.0 - is_last.astype(f32))
    earlier = lanes(1.0 - is_first.astype(f32))

    gather = gather_block if on_block else gather_any
    w_reduce, w_diff, w_pooled, w_spatial, w_expand, w_class = gather(
        reduce_weight, diff_weight, pooled_weight, spatial_weight, expand_weight, class_weight
    )

    tall = (clips, FRAME_ROWS, MID)
    tall_wide = (clips, FRAME_ROWS, D)
    narrow_note = shaped((devices, 8, MID // 4))
    wide_note = shaped((devices, 8, D // 4))
    packed = shaped((grid.total, MID), bf16)
    in_grid = shaped((grid.rows, MID))
    natural = pltpu.VMEM((4, clips * FRAME_ROWS, 128), f32)
    field = pltpu.VMEM((grid.total + 8, MID), f32)
    alive_in = (alive, SCALARS)
    counts_in = (counts, WHOLE)
    whole = lambda *arrays: [(array, WHOLE) for array in arrays]
    per_clip = lambda *arrays: [(array, each_clip(array.shape)) for array in arrays]
    vector_scratch = [pltpu.VMEM((clips, 1, MID), f32)] * 2

    first, note = call(
        first_kernel, "first", [alive_in, *per_clip(clips_in), *whole(w_reduce)],
        [*per_clip(shaped(tall)), *whole(narrow_note)], vector_scratch, clips,
    )
    got = exchange(note)
    norm_one, hidden, gating, diff_even, diff_odd, boost_even, boost_odd, summary = call(
        gate_kernel, "gate",
        [*whole(got, counts, first, g_one, s_one, following, later), (w_diff, ANY), (w_pooled, WHOLE)],
        whole(shaped((2, MID)), in_grid, in_grid, packed, packed, packed, packed, shaped((planes, MID))),
        [natural, field, pltpu.VMEM((9 * MID, MID), bf16), pltpu.SemaphoreType.DMA],
    )
    second, note = call(
        spatial_kernel, "spatial", [alive_in, *whole(boost_even, boost_odd, w_spatial)],
        whole(shaped(tall), narrow_note), [natural, field],
    )
    got = exchange(note)
    norm_two, hidden_two, third, note = call(
        expand_kernel, "expand",
        [alive_in, *whole(got, counts), *per_clip(second), *whole(g_two, s_two, w_expand)],
        [*whole(shaped((2, MID))), *per_clip(shaped(tall, bf16), shaped(tall_wide)), *whole(wide_note)],
        [pltpu.VMEM((clips, 1, D), f32)] * 2, clips,
    )
    got = exchange(note)
    norm_three, normed, summed_grad, note, video_sums, grad_class = call(
        outcome_kernel, "outcome",
        [
            alive_in, *whole(got, counts), *per_clip(third, clips_in),
            *whole(g_three, s_three, logit_grad, w_class, members),
        ],
        [
            *whole(shaped((2, D))), *per_clip(shaped(tall_wide, bf16), shaped(tall_wide, bf16)),
            *whole(wide_note, shaped((videos_all, 256)), shaped((D, 256), bf16)),
        ],
        [pltpu.VMEM((8, D), f32), pltpu.VMEM((2, D), f32), pltpu.VMEM((8, D), f32), pltpu.VMEM((2, D), f32)],
        clips,
    )
    got = exchange(note)
    grad_expand, pre_two_grad, note, grads_three = call(
        third_kernel, "third",
        [
            alive_in, *whole(got, counts), *per_clip(normed, summed_grad), *whole(g_three, norm_three),
            *per_clip(hidden_two), *whole(w_expand), *per_clip(second), *whole(norm_two, g_two, s_two),
        ],
        [*whole(shaped((MID, D), bf16)), *per_clip(shaped(tall)), *whole(narrow_note, shaped((2, D)))],
        [
            pltpu.VMEM((MID, D), f32), pltpu.VMEM((2, MID), f32),
            pltpu.VMEM((FRAME_ROWS, D), bf16), pltpu.VMEM((3, D), f32),
        ],
        clips,
    )
    got = exchange(note)
    grads_two, low_even, low_odd, grad_spatial = call(
        second_kernel, "second",
        [alive_in, *whole(got, counts, pre_two_grad, second, norm_two, g_two, g_one, s_one, boost_even, boost_odd)],
        whole(shaped((2, MID)), packed, packed, shaped((9 * MID, MID), bf16)), [natural, field],
    )
    hidden_grad, gate_even, gate_odd, grad_pooled, summary_grad = call(
        boost_back_kernel, "boost_back",
        whole(low_even, low_odd, w_spatial, hidden, gating, summary, w_pooled),
        whole(in_grid, packed, packed, shaped((MID, MID), bf16), shaped((planes, MID))), [field],
    )
    (grad_diff,) = call(
        diff_kernel, "diff", whole(diff_even, diff_odd, gate_even), whole(shaped((9 * MID, MID), bf16))
    )
    pre_one_grad, note = call(
        diff_back_kernel, "diff_back",
        [
            alive_in,
            *whole(gate_even, gate_odd, w_diff, summary_grad, hidden_grad, first, norm_one, g_one, s_one),
            *whole(before, earlier, later),
        ],
        whole(shaped(tall), narrow_note), [natural, field],
    )
    got = exchange(note)
    grads_one, low, grad_reduce = call(
        reduce_kernel, "reduce",
        [
            alive_in, *whole(got, counts), *per_clip(pre_one_grad, first), *whole(norm_one, g_one),
            *per_clip(clips_in),
        ],
        [*whole(shaped((2, MID))), *per_clip(shaped(tall, bf16)), *whole(shaped((D, MID), bf16))],
        [pltpu.VMEM((D, MID), f32)], clips,
    )
    (clips_grad,) = call(
        input_kernel, "input", [*per_clip(low), *whole(w_reduce), *per_clip(summed_grad)],
        per_clip(shaped(tall_wide, bf16)), (), clips,
    )

    reduce = reduce_block if on_block else reduce_any
    *reduced, video_total = reduce(
        grad_reduce, grad_diff, grad_pooled, grad_spatial, grad_expand, grad_class, video_sums
    )
    place = lax.axis_index("fsdp") * rep_count + lax.axis_index("rep")
    own_counts = lax.dynamic_slice_in_dim(video_count, place * own_videos, own_videos)
    video_logits = video_total[:, :classes] / own_counts[:, None]

    def own_piece(grads, row):
        length = grads.shape[1] // fsdp_count
        return lax.dynamic_slice(grads, (row, lax.axis_index("fsdp") * length), (1, length))[0]

    return (
        video_logits,
        clips_grad,
        reduced[0],
        own_piece(grads_one, 1),
        own_piece(grads_one, 0),
        reduced[1],
        reduced[2],
        reduced[3],
        own_piece(grads_two, 1),
        own_piece(grads_two, 0),
        reduced[4],
        own_piece(grads_three, 1),
        own_piece(grads_three, 0),
        reduced[5][:, :classes],
    )


def solution(mesh):
    clips, weight, vector = P(EVERY, None, None), P("fsdp", None), P("fsdp")
    rows = P(EVERY, None)
    placed = (
        clips, P(EVERY), rows,
        weight, vector, vector,
        weight, weight, weight, vector, vector,
        weight, vector, vector,
        weight, rows,
    )
    return jax.shard_map(
        local,
        mesh=mesh,
        in_specs=placed,
        out_specs=(
            rows, clips,
            weight, vector, vector,
            weight, weight, weight, vector, vector,
            weight, vector, vector,
            weight,
        ),
        check_vma=False,
    )
```

```python
import functools

import jax
import jax.numpy as jnp
from jax import lax
from jax.experimental import pallas as pl
from jax.experimental.pallas import tpu as pltpu
from jax.sharding import PartitionSpec as P

D = 2048
MID = 512
EVERY = ("fsdp", "rep")

epsilon = 1e-05
f32 = jnp.float32
bf16 = jnp.bfloat16

SEGS = 8
SIDE = 7
PIXELS = SIDE * SIDE
FRAME_ROWS = SEGS * PIXELS
WIDE = SIDE + 1
VMEM_LIMIT = 58 * 2**20
SCALE = 6.0


class Grid:
    def __init__(self, clips):
        self.clips = clips
        self.planes = clips * SEGS
        self.rows = SIDE * WIDE * self.planes
        self.lead = -(-((WIDE + 1) * self.planes) // 16) * 16
        self.total = self.rows + 2 * self.lead
        self.offsets = [
            (WIDE * dy + dx) * self.planes for dy in (-1, 0, 1) for dx in (-1, 0, 1)
        ]

    @classmethod
    def of(cls, total):
        clips = 1
        while cls(clips).total < total:
            clips += 1
        return cls(clips)

    def tap(self, even, odd, tap, start, count):
        offset = self.offsets[tap]
        if offset % 16 == 0:
            return even[pl.ds(self.lead + start + offset, count), :]
        return odd[pl.ds(self.lead + start + offset - 8, count), :]

    def clear_edges(self, field):
        zeros = jnp.zeros((self.lead, MID), f32)
        field[pl.ds(0, self.lead), :] = zeros
        field[pl.ds(self.lead + self.rows, self.lead), :] = zeros
        field[pl.ds(self.total, 8), :] = zeros[:8]

    def pack(self, field, even, odd):
        step = self.total // 7

        @pl.loop(0, 7)
        def _(i):
            start = pl.multiple_of(i * step, 16)
            even[pl.ds(start, step), :] = field[pl.ds(start, step), :].astype(bf16)
            odd[pl.ds(start, step), :] = field[pl.ds(start + 8, step), :].astype(bf16)


def sigmoid(values):
    return 0.5 * jnp.tanh(0.5 * values) + 0.5


def quarters(ref, rows=slice(None)):
    return jnp.concatenate([ref[block, rows, :] for block in range(4)], axis=1)


def put_quarters(ref, rows, value):
    for block in range(4):
        ref[block, rows, :] = value[:, block * 128 : (block + 1) * 128]


def clip_pixel(clip, pixel):
    return pl.ds(clip * FRAME_ROWS + pixel, SEGS, stride=PIXELS)


def send_out(payload, low, high):
    count, _, lanes = payload.shape
    for row in range(4):
        for at, vector in ((row, low), (row + 4, high)):
            payload[:, at, :] = jnp.broadcast_to(
                vector[:, row * lanes : (row + 1) * lanes], (count, lanes)
            )


def received(got, at):
    return jnp.concatenate([got[:, row, :] for row in range(at, at + 4)], axis=1)


def joint_moments(got, counts):
    count = counts[...]
    population = jnp.sum(count, axis=0, keepdims=True)
    means, squares = received(got, 0), received(got, 4)
    center = jnp.sum(count * means, axis=0, keepdims=True) / population
    offset = means - center
    spread = jnp.sum(squares + count * offset * offset, axis=0, keepdims=True) / population
    return center, lax.rsqrt(spread + epsilon)


def own_moments(alive, means, squares):
    clips = len(means)
    alive_sum = sum(alive[clip] for clip in range(clips))
    mean = sum(alive[clip] * means[clip] for clip in range(clips)) / jnp.maximum(alive_sum, 1.0)
    square = 0.0
    for clip in range(clips):
        offset = means[clip] - mean
        square = square + alive[clip] * (squares[clip] + FRAME_ROWS * offset * offset)
    return mean, square


def clip_moments(values):
    mean = jnp.sum(values, axis=0, keepdims=True) * (1.0 / FRAME_ROWS)
    offset = values - mean
    return mean, jnp.sum(offset * offset, axis=0, keepdims=True)


def joint_sums(got, counts):
    population = jnp.sum(counts[...], axis=0, keepdims=True)
    total = jnp.sum(got[...], axis=0)
    low = jnp.concatenate([total[row : row + 1] for row in range(4)], axis=1)
    high = jnp.concatenate([total[row : row + 1] for row in range(4, 8)], axis=1)
    return low, high, low / population, high / population


def contract_rows(left, right):
    return lax.dot_general(left, right, (((0,), (0,)), ((), ())), preferred_element_type=f32)


def contract_lanes(left, right):
    return lax.dot_general(left, right, (((1,), (1,)), ((), ())), preferred_element_type=f32)


def dot(left, right):
    return jnp.dot(left, right, preferred_element_type=f32)


def first_kernel(at, alive, clips_in, *refs):
    quads, (first, payload, means, squares, weight, sems) = refs[:4], refs[4:]
    clip = pl.program_id(0)

    @pl.when(clip == 0)
    def _():
        wait_all(fetch(at, quads, 0, weight, sems))

    first[0] = dot(clips_in[0], weight[...])
    mean, square = clip_moments(first[0])
    means[clip] = mean
    squares[clip] = square

    @pl.when(clip == pl.num_programs(0) - 1)
    def _():
        count = means.shape[0]
        mean, square = own_moments(
            alive, [means[i] for i in range(count)], [squares[i] for i in range(count)]
        )
        send_out(payload, mean, square)


def difference_kernel(
    at, got, counts, first, gain, shift, following, later,
    norm, hidden, diff_even, diff_odd, summary, natural, field,
):
    grid = Grid(first.shape[0])
    center, scale = joint_moments(got, counts)
    norm[0:1] = center
    norm[1:2] = scale
    ratio = scale * gain[...]
    for clip in range(grid.clips):

        @pl.loop(0, SIDE)
        def _(part):
            rows = pl.ds(pl.multiple_of(part * 56, 8), 56)
            pre = (first[clip, rows, :] - center) * ratio + shift[...]
            value = pre * sigmoid(pre)
            put_quarters(natural, pl.ds(pl.multiple_of(clip * FRAME_ROWS + part * 56, 8), 56), value)

    grid.clear_edges(field)
    zeros = jnp.zeros((grid.planes, MID), f32)

    def spread_row(y, totals):
        base = pl.multiple_of(y * (WIDE * grid.planes), 8)
        totals = list(totals)
        for x in range(SIDE):
            for clip in range(grid.clips):
                place = base + x * grid.planes + clip * SEGS
                own = quarters(natural, clip_pixel(clip, y * SIDE + x))
                index = following[pl.ds(clip * SEGS, SEGS), :]
                after = jnp.concatenate(
                    [
                        jnp.take_along_axis(own[:, b * 128 : (b + 1) * 128], index, axis=0)
                        for b in range(4)
                    ],
                    axis=1,
                )
                step = (after - own) * later[pl.ds(clip * SEGS, SEGS), 0:1]
                step = step.astype(bf16).astype(f32)
                hidden[pl.ds(place, SEGS), :] = own
                field[pl.ds(grid.lead + place, SEGS), :] = step
                totals[clip] = totals[clip] + step
        edge = base + SIDE * grid.planes
        hidden[pl.ds(edge, grid.planes), :] = zeros
        field[pl.ds(grid.lead + edge, grid.planes), :] = zeros
        return tuple(totals)

    totals = lax.fori_loop(0, SIDE, spread_row, (zeros[:SEGS],) * grid.clips)
    mean = (jnp.concatenate(totals, axis=0) * (1.0 / PIXELS)).astype(bf16)
    summary[...] = mean.astype(f32)
    grid.pack(field, diff_even, diff_odd)


def gate_kernel(at, diff_even, diff_odd, summary, hidden, *refs):
    quads = refs[:4]
    gating, boost_even, boost_odd, field, weight, w_pooled, sems, more_sems = refs[4:]
    grid = Grid.of(diff_even.shape[0])
    copies = fetch(at, quads, 0, weight, sems) + fetch(at, quads, 576, w_pooled, more_sems)
    grid.clear_edges(field)
    wait_all(copies)
    pooled_term = dot(summary[...].astype(bf16), w_pooled[...])
    part = grid.rows // 2
    for start in (0, part):
        total = None
        for tap in range(9):
            term = dot(grid.tap(diff_even, diff_odd, tap, start, part), weight[pl.ds(tap * MID, MID), :])
            total = term if total is None else total + term
        gating[pl.ds(start, part), :] = total

    def boost(pixel):
        rows = pl.ds(pl.multiple_of(pixel * grid.planes, 8), grid.planes)
        gate = sigmoid(gating[rows, :] + pooled_term)
        gating[rows, :] = gate
        value = hidden[rows, :] * (1.0 + gate)
        field[pl.ds(pl.multiple_of(grid.lead + pixel * grid.planes, 8), grid.planes), :] = value

    pl.loop(0, SIDE * WIDE)(boost)
    grid.pack(field, boost_even, boost_odd)


def spatial_kernel(at, alive, boost_even, boost_odd, *refs):
    quads, (second, payload, natural, field, w_spatial, sems) = refs[:8], refs[8:]
    grid = Grid(second.shape[0])
    wait_all(fetch(at, quads, 0, w_spatial, sems))
    part = grid.rows // 2
    for start in (0, part):
        total = None
        for tap in range(9):
            term = dot(grid.tap(boost_even, boost_odd, tap, start, part), w_spatial[pl.ds(tap * MID, MID), :])
            total = term if total is None else total + term
        field[pl.ds(start, part), :] = total
    to_natural(grid, lambda at, clip: field[pl.ds(at, SEGS), :], natural)
    means, squares = [], []
    for clip in range(grid.clips):
        second[clip] = quarters(natural, pl.ds(clip * FRAME_ROWS, FRAME_ROWS))
        mean, square = clip_moments(second[clip])
        means.append(mean)
        squares.append(square)
    mean, square = own_moments(alive, means, squares)
    send_out(payload, mean, square)


def to_natural(grid, tile, natural):
    @pl.loop(0, SIDE)
    def _(y):
        for x in range(SIDE):
            for clip in range(grid.clips):
                at = pl.multiple_of(y * (WIDE * grid.planes), 8) + x * grid.planes + clip * SEGS
                put_quarters(natural, clip_pixel(clip, y * SIDE + x), tile(at, clip))


def expand_kernel(
    at, alive, got, counts, second, gain, shift, *refs
):
    quads, (norm, hidden, third, payload, w_expand, means, squares, w_sems) = refs[:8], refs[8:]
    clip = pl.program_id(0)
    center, scale = joint_moments(got, counts)

    @pl.when(clip == 0)
    def _():
        wait_all(fetch_expand(at, quads, w_expand, w_sems))
        norm[0:1] = center
        norm[1:2] = scale

    ratio = scale * gain[...]
    pre = (second[0] - center) * ratio + shift[...]
    hidden[0] = (pre * sigmoid(pre)).astype(bf16)
    third[0] = dot(hidden[0], w_expand[...])
    mean, square = clip_moments(third[0])
    means[clip] = mean
    squares[clip] = square

    @pl.when(clip == pl.num_programs(0) - 1)
    def _():
        count = means.shape[0]
        mean, square = own_moments(
            alive, [means[i] for i in range(count)], [squares[i] for i in range(count)]
        )
        send_out(payload, mean, square)


def outcome_kernel(
    at, alive, got, counts, third, clips_in, gain, shift, logit_grad, members, *refs
):
    quads, refs = refs[:8], refs[8:]
    norm, normed, summed_grad, payload, video_sums, grad_class, theirs, mine = refs[:8]
    w_class, pooled_grad, sums, pooled, moments, w_sems = refs[8:]
    clip = pl.program_id(0)

    @pl.when(clip == 0)
    def _():
        copies = fetch_class(at, quads, w_class, w_sems)
        center, scale = joint_moments(got, counts)
        wait_all(copies)
        norm[0:1] = center
        norm[1:2] = scale
        moments[0:1] = center
        moments[1:2] = scale
        pooled_grad[...] = contract_lanes(logit_grad[...], w_class[...]) * (1.0 / FRAME_ROWS)
        sums[...] = jnp.zeros_like(sums)
        pooled[...] = jnp.zeros_like(pooled)

    weight = alive[clip]
    for lane in range(0, D, 512):
        lanes = pl.ds(lane, 512)
        center, scale = moments[0:1, lanes], moments[1:2, lanes]
        g, s = gain[:, lanes], shift[:, lanes]
        slope_grad = pooled_grad[pl.ds(clip, 1), lanes]

        def piece(start, count, carry):
            rows = pl.ds(start, count)
            value = (third[0, rows, lanes] - center) * scale
            total = value * g + s + clips_in[0, rows, lanes].astype(f32)
            sigma = sigmoid(total)
            out = total * sigma
            grad = slope_grad * (sigma + out * (1.0 - sigma))
            normed[0, rows, lanes] = value.astype(bf16)
            summed_grad[0, rows, lanes] = grad.astype(bf16)
            eights = lambda v: jnp.sum(v.reshape(count // 8, 8, 512), axis=0)
            return (
                carry[0] + eights(grad),
                carry[1] + eights(grad * value),
                carry[2] + eights(out),
            )

        zero = jnp.zeros((8, 512), f32)
        carry = lax.fori_loop(
            0, FRAME_ROWS // 16, lambda i, c: piece(pl.multiple_of(i * 16, 16), 16, c), (zero,) * 3
        )
        tail = FRAME_ROWS - FRAME_ROWS % 16
        if tail < FRAME_ROWS:
            carry = piece(tail, FRAME_ROWS - tail, carry)
        low, high, mean = (jnp.sum(v, axis=0, keepdims=True) for v in carry)
        sums[0:1, lanes] = sums[0:1, lanes] + weight * low
        sums[1:2, lanes] = sums[1:2, lanes] + weight * high
        pooled[pl.ds(clip, 1), lanes] = mean * (1.0 / FRAME_ROWS)

    @pl.when(clip == pl.num_programs(0) - 1)
    def _():
        send_out(payload, sums[0:1], sums[1:2])
        rounded = pooled[...].astype(bf16)
        logits = dot(rounded, w_class[...])
        total = 0.0
        for i in range(clips_of(members)):
            total = total + members[:, i : i + 1] * logits[i : i + 1]
        video_sums[...] = total
        grad_class[...] = contract_rows(rounded, logit_grad[...]).astype(bf16)
        for shard in range(8):
            for out, core in ((theirs, 1 - at[1]), (mine, at[1])):
                rows = pl.ds(pl.multiple_of(shard * 256 + core * 128, 128), 128)
                out[shard, 0:128, :] = grad_class[rows, :]
                videos = [video_sums[pl.ds(shard * 4 + x * 2 + core, 1), :] for x in (0, 1)]
                videos += [jnp.zeros((14, 256), f32)]
                out[shard, 128:144, :] = jnp.concatenate(videos).astype(bf16)


def clips_of(members):
    return members.shape[1]


def third_kernel(
    at, alive, got, counts, normed, summed_grad, gain, norm_three, hidden, second, norm_two, gain_two, shift_two,
    *refs,
):
    quads, refs = refs[:8], refs[8:]
    theirs, mine, pre_grad, payload, grads, w_expand, total, sums, low, columns, w_sems = refs
    clip = pl.program_id(0)

    @pl.when(clip == 0)
    def _():
        wait_all(fetch_expand(at, quads, w_expand, w_sems))
        total[...] = jnp.zeros_like(total)
        columns[...] = jnp.zeros_like(columns)
        sums[...] = jnp.zeros_like(sums)
        shift_grad, gain_grad, shift_share, gain_share = joint_sums(got, counts)
        grads[0:1] = shift_grad
        grads[1:2] = gain_grad
        columns[1:2] = shift_share
        columns[2:3] = gain_share

    weight = alive[clip]
    ratio = gain[...] * norm_three[1:2]
    for lane in range(0, D, 512):
        lanes = pl.ds(lane, 512)
        shift_share, gain_share = columns[1:2, lanes] * weight, columns[2:3, lanes] * weight
        r = ratio[:, lane : lane + 512]

        def piece(start, count, carry):
            rows = pl.ds(start, count)
            value = summed_grad[0, rows, lanes].astype(f32) - (
                shift_share + normed[0, rows, lanes].astype(f32) * gain_share
            )
            value = (r * value).astype(bf16)
            low[rows, lanes] = value
            return carry + jnp.sum(value.astype(f32).reshape(count // 8, 8, 512), axis=0)

        carry = lax.fori_loop(
            0,
            FRAME_ROWS // 16,
            lambda i, c: piece(pl.multiple_of(i * 16, 16), 16, c),
            jnp.zeros((8, 512), f32),
        )
        tail = FRAME_ROWS - FRAME_ROWS % 16
        if tail < FRAME_ROWS:
            carry = piece(tail, FRAME_ROWS - tail, carry)
        columns[0:1, lanes] = columns[0:1, lanes] + jnp.sum(carry, axis=0, keepdims=True)
    grad_out = low[pl.ds(0, FRAME_ROWS), :]
    total[...] = total[...] + contract_rows(hidden[0], grad_out)
    back = contract_lanes(grad_out, w_expand[...])
    value = (second[0] - norm_two[0:1]) * norm_two[1:2]
    pre = value * gain_two[...] + shift_two[...]
    sigma = sigmoid(pre)
    grad = back * (sigma * (1.0 + pre * (1.0 - sigma)))
    pre_grad[0] = grad
    sums[0:1] = sums[0:1] + weight * jnp.sum(grad, axis=0, keepdims=True)
    sums[1:2] = sums[1:2] + weight * jnp.sum(grad * value, axis=0, keepdims=True)

    @pl.when(clip == pl.num_programs(0) - 1)
    def _():
        send_out(payload, sums[0:1], sums[1:2])
        mean = usual_silu(shift_two[...], gain_two[...])
        offset = outer(mean, columns[0:1])
        total[...] = total[...] - offset
        core = at[1]
        theirs[...] = total[:, core_lanes(1 - core, D // 2)].astype(bf16)
        mine[...] = total[:, core_lanes(core, D // 2)].astype(bf16)


def usual_silu(shift, gain):
    silu = lambda v: v * sigmoid(v)
    wide = 3.0**0.5 * gain
    return (2.0 / 3.0) * silu(shift) + (silu(shift + wide) + silu(shift - wide)) * (1.0 / 6.0)


def outer(column, row):
    return jnp.swapaxes(jnp.broadcast_to(column, (8, column.shape[1])), 0, 1)[:, 0:1] * row


def to_grid(grid, natural, put):
    @pl.loop(0, SIDE)
    def _(y):
        base = pl.multiple_of(y * (WIDE * grid.planes), 8)
        for x in range(SIDE):
            for clip in range(grid.clips):
                put(base + x * grid.planes + clip * SEGS, clip, quarters(natural, clip_pixel(clip, y * SIDE + x)))
        put(base + SIDE * grid.planes, None, jnp.zeros((grid.planes, MID), f32))


def second_kernel(
    at, alive, got, counts, pre_grad, second, norm_two, gain_two, gain_one, shift_one, boost_even, boost_odd,
    grads, low_even, low_odd, theirs0, theirs1, theirs2, offset, natural, field,
):
    grid = Grid(pre_grad.shape[0])
    shift_grad, gain_grad, shift_share, gain_share = joint_sums(got, counts)
    grads[0:1] = shift_grad
    grads[1:2] = gain_grad
    center, scale = norm_two[0:1], norm_two[1:2]
    ratio = gain_two[...] * scale
    columns = jnp.zeros((8, MID), f32)
    for clip in range(grid.clips):
        weight = alive[clip]

        def piece(part, columns):
            rows = pl.ds(pl.multiple_of(part * 56, 8), 56)
            value = (second[clip, rows, :] - center) * scale
            grad = ratio * (pre_grad[clip, rows, :] - weight * (shift_share + value * gain_share))
            grad = grad.astype(bf16).astype(f32)
            put_quarters(natural, pl.ds(pl.multiple_of(clip * FRAME_ROWS + part * 56, 8), 56), grad)
            return columns + jnp.sum(grad.reshape(7, 8, MID), axis=0)

        columns = lax.fori_loop(0, SIDE, piece, columns)
    columns = jnp.sum(columns, axis=0, keepdims=True)
    grid.clear_edges(field)

    def put(at, clip, value):
        field[pl.ds(grid.lead + at, value.shape[0]), :] = value

    to_grid(grid, natural, put)
    grid.pack(field, low_even, low_odd)
    offset[...] = outer(1.5 * usual_silu(shift_one[...], gain_one[...]), columns)
    lanes = core_lanes(1 - at[1], MID // 2)
    grad_out = low_even[pl.ds(grid.lead, grid.rows), lanes]
    for tap in range(9):
        term = contract_rows(grid.tap(boost_even, boost_odd, tap, 0, grid.rows), grad_out)
        theirs = (theirs0, theirs1, theirs2)[tap // 3]
        theirs[pl.ds(tap % 3 * MID, MID), :] = (term - offset[:, lanes]).astype(bf16)


def own_spatial_kernel(
    at, boost_even, boost_odd, low_even, offset, there0, there1, there2, sent, kept, total
):
    grid = Grid.of(low_even.shape[0])
    lanes = core_lanes(at[1], MID // 2)
    grad_out = low_even[pl.ds(grid.lead, grid.rows), lanes]
    for tap in range(9):
        rows = pl.ds(tap * MID, MID)
        term = contract_rows(grid.tap(boost_even, boost_odd, tap, 0, grid.rows), grad_out)
        there = (there0, there1, there2)[tap // 3][pl.ds(tap % 3 * MID, MID), :]
        total[...] = (term - offset[:, lanes] + there.astype(f32)).astype(bf16)
        sent[rows, :] = total[:, core_lanes(1 - at[3], 128)]
        kept[rows, :] = total[:, core_lanes(at[3], 128)]


def boost_back_kernel(at, low_even, low_odd, hidden, gating, summary, *refs):
    spatial_quads, diff_quads = refs[:8], refs[8:12]
    hidden_grad, gate_even, gate_odd, pooled_theirs, pooled_mine, summary_grad = refs[12:18]
    field, w_spatial, w_pooled, sems, more_sems = refs[18:]
    copies = fetch(at, spatial_quads, 0, w_spatial, sems) + fetch(at, diff_quads, 576, w_pooled, more_sems)
    wait_all(copies)
    grid = Grid(hidden.shape[0] // (SIDE * WIDE * SEGS))
    part = grid.rows // 2
    for start in (0, part):
        total = None
        for tap in range(9):
            term = contract_lanes(
                grid.tap(low_even, low_odd, 8 - tap, start, part), w_spatial[pl.ds(tap * MID, MID), :]
            )
            total = term if total is None else total + term
        hidden_grad[pl.ds(start, part), :] = total
    grid.clear_edges(field)

    def piece(pixel, total):
        rows = pl.ds(pl.multiple_of(pixel * grid.planes, 8), grid.planes)
        grad, gate = hidden_grad[rows, :], gating[rows, :]
        hidden_grad[rows, :] = grad * (1.0 + gate)
        gate_grad = (grad * hidden[rows, :] * gate * (1.0 - gate)).astype(bf16).astype(f32)
        field[pl.ds(pl.multiple_of(grid.lead + pixel * grid.planes, 8), grid.planes), :] = gate_grad
        return total + gate_grad

    gate_sums = lax.fori_loop(0, SIDE * WIDE, piece, jnp.zeros((grid.planes, MID), f32))
    grid.pack(field, gate_even, gate_odd)
    high = gate_sums.astype(bf16)
    low = (gate_sums - high.astype(f32)).astype(bf16)
    mean = summary[...].astype(bf16)
    grad_pooled = contract_rows(mean, high) + contract_rows(mean, low)
    field[pl.ds(0, MID), :] = grad_pooled
    core = at[1]
    pooled_theirs[...] = field[pl.ds(0, MID), core_lanes(1 - core, MID // 2)].astype(bf16)
    pooled_mine[...] = field[pl.ds(0, MID), core_lanes(core, MID // 2)].astype(bf16)
    back = contract_lanes(high, w_pooled[...]) + contract_lanes(low, w_pooled[...])
    summary_grad[...] = back * (1.0 / PIXELS)


def their_diff_kernel(at, diff_even, diff_odd, gate_even, pooled, *theirs):
    grid = Grid.of(gate_even.shape[0])
    grad_out = gate_even[pl.ds(grid.lead, grid.rows), core_lanes(1 - at[1], MID // 2)]
    for tap in range(9):
        term = contract_rows(grid.tap(diff_even, diff_odd, tap, 0, grid.rows), grad_out)
        theirs[tap // 4][pl.ds(tap % 4 * MID, MID), :] = term.astype(bf16)
    theirs[2][pl.ds(MID, MID), :] = pooled[...]


def own_diff_kernel(
    at, diff_even, diff_odd, gate_even, pooled, there0, there1, there2, sent, kept, total
):
    grid = Grid.of(gate_even.shape[0])
    grad_out = gate_even[pl.ds(grid.lead, grid.rows), core_lanes(at[1], MID // 2)]
    for tap in range(10):
        rows = pl.ds(tap * MID, MID)
        if tap < 9:
            term = contract_rows(grid.tap(diff_even, diff_odd, tap, 0, grid.rows), grad_out)
        else:
            term = pooled[...].astype(f32)
        there = (there0, there1, there2)[tap // 4][pl.ds(tap % 4 * MID, MID), :]
        total[...] = (term + there.astype(f32)).astype(bf16)
        sent[rows, :] = total[:, core_lanes(1 - at[3], 128)]
        kept[rows, :] = total[:, core_lanes(at[3], 128)]


def diff_back_kernel(
    at, alive, gate_even, gate_odd, summary_grad, hidden_grad, first, norm_one, gain, shift, before, earlier, later,
    *refs,
):
    quads, (pre_grad, payload, natural, field, w_diff, sems) = refs[:4], refs[4:]
    grid = Grid(first.shape[0])
    wait_all(fetch(at, quads, 0, w_diff, sems))
    part = grid.rows // 2
    for start in (0, part):
        total = None
        for tap in range(9):
            term = contract_lanes(
                grid.tap(gate_even, gate_odd, 8 - tap, start, part), w_diff[pl.ds(tap * MID, MID), :]
            )
            total = term if total is None else total + term
        field[pl.ds(start, part), :] = total

    def tile(at, clip):
        planes = pl.ds(clip * SEGS, SEGS)
        grad = field[pl.ds(at, SEGS), :] + summary_grad[planes, :]
        index = before[planes, :]
        back = jnp.concatenate(
            [
                jnp.take_along_axis(grad[:, b * 128 : (b + 1) * 128], index, axis=0)
                for b in range(4)
            ],
            axis=1,
        )
        own = hidden_grad[pl.ds(at, SEGS), :]
        return own + back * earlier[planes, 0:1] - grad * later[planes, 0:1]

    to_natural(grid, tile, natural)
    center, scale = norm_one[0:1], norm_one[1:2]
    low = jnp.zeros((8, MID), f32)
    high = jnp.zeros((8, MID), f32)
    for clip in range(grid.clips):
        weight = alive[clip]

        def piece(step, carry):
            rows = pl.ds(pl.multiple_of(step * 56, 8), 56)
            value = (first[clip, rows, :] - center) * scale
            pre = value * gain[...] + shift[...]
            sigma = sigmoid(pre)
            grad = quarters(natural, pl.ds(pl.multiple_of(clip * FRAME_ROWS + step * 56, 8), 56))
            grad = grad * (sigma * (1.0 + pre * (1.0 - sigma)))
            pre_grad[clip, rows, :] = grad
            eights = lambda v: jnp.sum(v.reshape(7, 8, MID), axis=0) * weight
            return carry[0] + eights(grad), carry[1] + eights(grad * value)

        low, high = lax.fori_loop(0, SIDE, piece, (low, high))
    send_out(payload, jnp.sum(low, axis=0, keepdims=True), jnp.sum(high, axis=0, keepdims=True))


def reduce_kernel(
    at, alive, got, counts, pre_grad, first, norm_one, gain, clips_in,
    grads, low, theirs0, theirs1, mine, total,
):
    clip = pl.program_id(0)
    shift_grad, gain_grad, shift_share, gain_share = joint_sums(got, counts)

    @pl.when(clip == 0)
    def _():
        total[...] = jnp.zeros_like(total)
        grads[0:1] = shift_grad
        grads[1:2] = gain_grad

    center, scale = norm_one[0:1], norm_one[1:2]
    value = (first[0] - center) * scale
    grad = pre_grad[0] - alive[clip] * (shift_share + value * gain_share)
    low[0] = (gain[...] * scale * grad).astype(bf16)
    total[...] = total[...] + contract_rows(clips_in[0], low[0])

    @pl.when(clip == pl.num_programs(0) - 1)
    def _():
        core = at[1]
        lanes = core_lanes(1 - core, MID // 2)
        theirs0[...] = total[pl.ds(0, D // 2), lanes].astype(bf16)
        theirs1[...] = total[pl.ds(D // 2, D // 2), lanes].astype(bf16)
        mine[...] = total[:, core_lanes(core, MID // 2)].astype(bf16)


def input_kernel(at, low, *refs):
    quads, (summed_grad, clips_grad, weight, sems) = refs[:4], refs[4:]

    @pl.when(pl.program_id(0) == 0)
    def _():
        wait_all(fetch(at, quads, 0, weight, sems))

    back = contract_lanes(low[0], weight[...])
    clips_grad[0] = (back + summed_grad[0].astype(f32)).astype(bf16)


def cut_kernel(
    at, reduce_weight, diff_weight, pooled_weight, spatial_weight, expand_weight, class_weight,
    low, middle, high,
):
    core = at[1]
    lanes = core_lanes(core, MID // 2)
    low[...] = reduce_weight[:, lanes]
    middle[0:576, :] = diff_weight[:, lanes]
    middle[576:640, :] = pooled_weight[:, lanes]
    x = at[3]
    quarter = lambda start: pl.ds(pl.multiple_of(start + x * 128, 128), 128)
    high[0:576, :] = spatial_weight[:, quarter(core * 256)]
    for block in range(4):
        high[576 + 64 * block : 640 + 64 * block, :] = expand_weight[:, quarter(core * 1024 + block * 256)]
    rows = pl.ds(pl.multiple_of(core * 128 + x * 64, 64), 64)
    high[832:896, :] = class_weight[rows, 0:128]
    high[896:960, :] = class_weight[rows, 128:256]


def stack_kernel(at, *refs):
    pieces, outs = refs[:4], refs[4:]
    start = 0
    for out in outs:
        rows = out.shape[1]
        for hop in range(4):
            out[jnp.bitwise_xor(at[2], hop)] = pieces[hop][pl.ds(start, rows), :]
        start += rows


def expand_cut_kernel(at, expand_mine, expand_there, class_mine, class_there, sent, kept):
    for z in range(4):
        for out, row in ((sent, 1 - at[0]), (kept, at[0])):
            shard = z * 2 + row
            rows = pl.ds(pl.multiple_of(shard * 64, 64), 64)
            value = expand_mine[rows, :].astype(f32) + expand_there[rows, :].astype(f32)
            for block in range(4):
                out[z, 64 * block : 64 * (block + 1), :] = value[
                    :, 256 * block : 256 * (block + 1)
                ].astype(bf16)
            value = class_mine[shard].astype(f32) + class_there[shard].astype(f32)
            out[z, 256:400, :] = value.astype(bf16)


def totals_kernel(counts, at, *refs):
    out, index, start = refs[-1], 0, 0
    for count in counts:
        value = sum(ref[...].astype(f32) for ref in refs[index : index + count])
        rows, lanes = value.shape
        if lanes == 128:
            rows //= 2
            value = jnp.concatenate([value[:rows], value[rows:]], axis=1)
        out[pl.ds(start, rows), :] = value.astype(bf16)
        index, start = index + count, start + rows


def meet_kernel(at, total, there, out):
    mine, other = total[0:400, :].astype(f32), there[0:400, :].astype(f32)
    out[0:400, :] = (mine + other).astype(bf16)
    start, place = 400, 400
    for rows in (320, 288):
        for ref, x in ((total, at[3]), (there, 1 - at[3])):
            for part in (0, 1):
                out[pl.ds(place + rows * part, rows), core_lanes(x, 128)] = ref[
                    pl.ds(start, rows), 128 * part : 128 * (part + 1)
                ]
        start, place = start + rows, place + 2 * rows


def finish_kernel(at, total, there, grad_expand, grad_class, videos, grad_diff, grad_pooled, grad_spatial):
    for array, core in ((total, at[1]), (there, 1 - at[1])):
        for block in range(4):
            place = pl.ds(pl.multiple_of(core * 1024 + block * 256, 256), 256)
            grad_expand[:, place] = array[64 * block : 64 * (block + 1), :].astype(f32)
        grad_class[pl.ds(pl.multiple_of(core * 128, 128), 128), :] = array[256:384, :].astype(f32)
        place = core_lanes(core, 256)
        grad_diff[:, place] = array[400:976, :].astype(f32)
        grad_pooled[:, place] = array[976:1040, :].astype(f32)
        grad_spatial[:, place] = array[1040:1616, :].astype(f32)
    videos[...] = total[384:400, :].astype(f32)


def fold_kernel(at, kept, there, own, *sent):
    for hop, out in enumerate((own, *sent)):
        z = jnp.bitwise_xor(at[2], hop)
        out[...] = (kept[z].astype(f32) + there[z].astype(f32)).astype(bf16)


def core_lanes(core, width):
    return pl.ds(pl.multiple_of(core * width, width), width)


def fetch(at, quads, start, weight, sems):
    count = weight.shape[0] // 8
    jobs = []
    for quad, shard, core, x in quad_places(at, quads):
        rows = pl.ds(pl.multiple_of(shard * count, 16), count)
        width = quad.shape[1]
        lanes = pl.ds(pl.multiple_of(core * 256 + x * 128, width), width)
        jobs.append((quad.at[pl.ds(start, count), :], weight.at[rows, lanes]))
    return start_all(jobs, sems)


def quad_places(at, quads):
    half = len(quads) // 2
    for index, quad in enumerate(quads):
        row = at[0] if index % 2 == 0 else 1 - at[0]
        core = at[1] if index < half else 1 - at[1]
        x = 0
        if half == 4:
            x = at[3] if index % 4 < 2 else 1 - at[3]
        for z in range(4):
            yield quad.at[z], z * 2 + row, core, x


def fetch_expand(at, quads, weight, sems):
    jobs = []
    for quad, shard, core, x in quad_places(at, quads):
        for block in range(4):
            place = pl.ds(pl.multiple_of(core * 1024 + block * 256 + x * 128, 128), 128)
            rows = pl.ds(pl.multiple_of(shard * 64, 64), 64)
            jobs.append((quad.at[pl.ds(64 * block, 64), :], weight.at[rows, place]))
    return start_all(jobs, sems)


def fetch_class(at, quads, weight, sems):
    jobs = []
    for quad, shard, core, x in quad_places(at, quads):
        rows = pl.ds(pl.multiple_of(shard * 256 + core * 128 + x * 64, 64), 64)
        for block in range(2):
            source = quad.at[pl.ds(256 + 64 * block, 64), :]
            jobs.append((source, weight.at[rows, pl.ds(128 * block, 128)]))
    return start_all(jobs, sems)


def start_all(jobs, sems):
    copies = [pltpu.make_async_copy(*job, sems.at[i]) for i, job in enumerate(jobs)]
    for copy in copies:
        copy.start()
    return copies


def wait_all(copies):
    for copy in copies:
        copy.wait()


def split_kernel(sizes, at, mine, *refs):
    theres, (sent, kept) = refs[:-2], refs[-2:]
    for z in range(4):
        there = theres[z * len(theres) // 4]
        for out, row in ((sent, 1 - at[0]), (kept, at[0])):
            start = place = 0
            for size in sizes:
                rows = pl.ds(pl.multiple_of(start + (z * 2 + row) * size, 16), size)
                first = z * len(theres) // 4 * mine.shape[0] // len(theres)
                there_rows = pl.ds(pl.multiple_of(start + (z * 2 + row) * size - first, 16), size)
                value = mine[rows, :].astype(f32) + there[there_rows, :].astype(f32)
                out[z, pl.ds(place, size), :] = value.astype(bf16)
                start, place = start + 8 * size, place + size


def join_kernel(at, mine, there, *outs):
    start = 0
    for out in outs:
        rows, lanes = out.shape
        for block in range(lanes // 512):
            for array, core in ((mine, at[1]), (there, 1 - at[1])):
                place = pl.ds(pl.multiple_of(core * (lanes // 2) + block * 256, 256), 256)
                out[:, place] = array[pl.ds(start + block * rows, rows), :].astype(f32)
        start += rows * (lanes // 512)


SCALARS = pl.BlockSpec(memory_space=pltpu.SMEM)
WHOLE = pl.BlockSpec(memory_space=pltpu.VMEM)


def each_clip(shape):
    return pl.BlockSpec((1, *shape[1:]), lambda clip: (clip, 0, 0))


def shaped(shape, dtype=f32):
    return jax.ShapeDtypeStruct(tuple(shape), dtype)


def whole(*arrays):
    return [(array, WHOLE) for array in arrays]


def anywhere(*arrays):
    return [(array, pl.BlockSpec(memory_space=pl.ANY)) for array in arrays]


def per_clip(*arrays):
    return [(array, each_clip(array.shape)) for array in arrays]


def dma(count):
    return pltpu.SemaphoreType.DMA((count,))


class Chain:
    def __init__(self, place):
        self.at = jnp.stack([jnp.asarray(part, jnp.int32) for part in place])

    def __call__(self, kernel, name, micros, ins, outs, scratch=(), clips=None, after=()):
        skip = 1 + len(after)
        last = skip + len(ins) + len(outs)

        def body(*refs):
            for index in range(4):
                refs[last][index] = refs[0][index]
            kernel(refs[0], *refs[skip:last], *refs[last + 1 :])

        results = pl.pallas_call(
            body,
            out_shape=[*[shape for shape, _ in outs], shaped((4,), jnp.int32)],
            grid=(clips,) if clips else (),
            in_specs=[SCALARS, *[spec for _, spec in anywhere(*after)], *[spec for _, spec in ins]],
            out_specs=[*[spec for _, spec in outs], SCALARS],
            scratch_shapes=list(scratch),
            compiler_params=pltpu.CompilerParams(vmem_limit_bytes=VMEM_LIMIT),
            cost_estimate=pl.CostEstimate(
                flops=int(micros * SCALE * 1.1e9), bytes_accessed=int(micros * SCALE * 3.6e6), transcendentals=0
            ),
            name=name,
        )(self.at, *after, *[array for array, _ in ins])
        self.at = results[-1]
        return results[:-1]

    def hold(self, array):
        return lax.optimization_barrier((array, self.at))[0]


def exchange(payload):
    return lax.all_to_all(payload, EVERY, 0, 0, tiled=True)


def swap(array, bit):
    count = lax.axis_size("fsdp") * lax.axis_size("rep")
    return lax.ppermute(array, EVERY, [(place, place ^ bit) for place in range(count)])


CORE, X, Y, Z = 1, 2, 4, 8


class Block:
    def __init__(self):
        place = lax.axis_index("fsdp") * 4 + lax.axis_index("rep")
        self.run = Chain([(place >> 2) & 1, place & 1, place >> 3, (place >> 1) & 1])

    def cut(self, *shards):
        sizes = ((256, 256), (640, 256), (960, 128))
        return self.run(cut_kernel, "cut", 3, whole(*shards), whole(*[shaped(size, bf16) for size in sizes]))

    def along_z(self, piece):
        return (piece, *[swap(piece, hop * Z) for hop in (1, 2, 3)])

    def stack(self, micros, pieces, *sizes, after=()):
        rows, lanes = pieces[0].shape
        shapes = [shaped((4, size, lanes), bf16) for size in sizes or (rows,)]
        return self.run(stack_kernel, "stack", micros, whole(*pieces), whole(*shapes), after=after)

    def across(self, own):
        return own, swap(own, Y)

    def complete(self, own, across):
        return anywhere(own, across, swap(own, CORE), swap(across, CORE))

    def complete_quarters(self, *mine):
        return anywhere(*mine, *[swap(part, CORE) for part in mine])

    def across_both(self, own):
        return own, swap(own, Y), swap(own, X)

    def across_again(self, own, across, over_x):
        return own, across, over_x, swap(across, X)

    def by_y(self, mine, theres, *sizes):
        half = shaped((4, sum(sizes), mine.shape[1]), bf16)
        kernel = functools.partial(split_kernel, sizes)
        return self.run(kernel, "split", 3, whole(mine, *theres), whole(half, half))

    def fold(self, kept, there):
        rows = shaped(kept.shape[1:], bf16)
        own, *others = self.run(fold_kernel, "fold", 3, whole(kept, there), whole(rows, rows, rows, rows))
        return own, *[swap(other, hop * Z) for hop, other in zip((1, 2, 3), others)]

    def totals(self, *groups):
        refs = [ref for group in groups for ref in group]
        rows = sum(group[0].shape[0] * group[0].shape[1] // 256 for group in groups)
        kernel = functools.partial(totals_kernel, [len(group) for group in groups])
        return self.run(kernel, "totals", 2, whole(*refs), whole(shaped((rows, 256), bf16)))[0]


class Anywhere:
    def __init__(self):
        self.run = Chain([0, 0, 0, 0])

    def cut(self, *shards):
        reduce_weight, diff, pooled, spatial, expand, classes = [
            lax.all_gather(shard, "fsdp", axis=0, tiled=True) for shard in shards
        ]
        low, diff, pooled, high = [
            array.reshape(4, 2, -1, 2, 256) for array in (reduce_weight, diff, pooled, spatial)
        ]
        middle = jnp.concatenate([diff, pooled], axis=2)
        high = high.reshape(4, 2, 576, 2, 2, 128)
        expand = expand.reshape(4, 2, 64, 2, 4, 2, 128)
        expand = jnp.moveaxis(expand, 4, 2).reshape(4, 2, 256, 2, 2, 128)
        classes = classes.reshape(4, 2, 2, 2, 64, 2, 128)
        classes = jnp.transpose(classes, (0, 1, 5, 4, 2, 3, 6)).reshape(4, 2, 128, 2, 2, 128)
        return low, middle, jnp.concatenate([high, expand, classes], axis=2)

    def along_z(self, piece):
        return piece

    def stack(self, micros, piece, *sizes, after=()):
        cuts = [sum(sizes[:count]) for count in range(1, len(sizes))]
        return jnp.split(piece, cuts, axis=2)

    def across(self, piece):
        return (piece,)

    def across_both(self, piece):
        return (piece,)

    def across_again(self, piece):
        return (piece,)

    def complete(self, piece):
        return anywhere(*[piece[:, y, :, core] for core in (0, 1) for y in (0, 1)])

    def complete_quarters(self, piece):
        return anywhere(
            *[piece[:, y, :, core, x] for core in (0, 1) for x in (0, 1) for y in (0, 1)]
        )

    def scatter(self, lower, upper):
        grads = jnp.concatenate([lower, upper], axis=1)
        return self.scatter_rows(grads)

    def scatter_rows(self, grads):
        grads = grads.astype(f32)
        return lax.psum(lax.psum_scatter(grads, "fsdp", scatter_dimension=0, tiled=True), "rep")

    def both_x(self, sent, kept):
        return jnp.concatenate([kept, sent], axis=1)


def local(
    clips_in,
    view_ids,
    seg_order,
    reduce_weight,
    gain1,
    shift1,
    diff_weight,
    pooled_weight,
    spatial_weight,
    gain2,
    shift2,
    expand_weight,
    gain3,
    shift3,
    class_weight,
    video_cotangent,
):
    fsdp_count = lax.axis_size("fsdp")
    rep_count = lax.axis_size("rep")
    devices = fsdp_count * rep_count
    clips = clips_in.shape[0]
    own_videos, classes = video_cotangent.shape
    videos_all = own_videos * devices
    on_block = (fsdp_count, rep_count) == (8, 4)
    grid = Grid(clips)
    planes = grid.planes

    vectors = (gain1, shift1, gain2, shift2, gain3, shift3)
    early = [view_ids.astype(f32), video_cotangent.reshape(-1)]
    early += [vector.astype(f32) for vector in vectors]
    early = jnp.concatenate(early)
    room = -(-early.shape[0] // 1024) * 1024
    early = jnp.pad(early, (0, room - early.shape[0])).reshape(1, 8, room // 8)
    early = jnp.broadcast_to(early, (devices, 8, room // 8))

    moves = Block() if on_block else Anywhere()
    run = moves.run
    wide_class = jnp.pad(class_weight, ((0, 0), (0, 256 - classes)))
    pieces = moves.cut(
        reduce_weight, diff_weight, pooled_weight, spatial_weight, expand_weight, wide_class
    )

    alive = (view_ids < videos_all).astype(f32)
    video_list = jnp.arange(videos_all, dtype=jnp.int32)
    members = (video_list[:, None] == view_ids[None, :]).astype(f32)

    stations = jnp.arange(SEGS, dtype=jnp.int32)
    places = (seg_order[:, :, None] == stations).astype(jnp.int32)
    place = jnp.sum(places * stations[None, :, None], axis=1)
    is_last, is_first = place == SEGS - 1, place == 0
    at = lambda wanted: jnp.sum(
        (jnp.clip(wanted, 0, SEGS - 1)[:, :, None] == stations).astype(jnp.int32)
        * seg_order[:, None, :],
        axis=2,
    )
    lanes = lambda array: jnp.broadcast_to(array.reshape(planes, 1), (planes, 128))
    following = lanes(at(place + 1))
    before = lanes(at(place - 1))
    later = lanes(1.0 - is_last.astype(f32))
    earlier = lanes(1.0 - is_first.astype(f32))

    low, middle = moves.along_z(pieces[0]), moves.along_z(pieces[1])
    stack_reduce = moves.across(*moves.stack(2, low))
    stack_diff = moves.across(*moves.stack(30, middle))
    high = moves.along_z(run.hold(pieces[2]))
    quad_reduce = moves.complete(*stack_reduce)

    tall = (clips, FRAME_ROWS, MID)
    tall_wide = (clips, FRAME_ROWS, D)
    narrow_note = shaped((devices, 8, MID // 4))
    wide_note = shaped((devices, 8, D // 4))
    packed = shaped((grid.total, MID), bf16)
    in_grid = shaped((grid.rows, MID))
    natural = pltpu.VMEM((4, clips * FRAME_ROWS, 128), f32)
    field = pltpu.VMEM((grid.total + 8, MID), f32)
    alive_in = (alive, SCALARS)
    vector_scratch = [pltpu.VMEM((clips, 1, MID), f32)] * 2

    w_mid = pltpu.VMEM((9 * MID, MID), bf16)
    w_small = pltpu.VMEM((MID, MID), bf16)
    w_wide = pltpu.VMEM((MID, D), bf16)

    first, note = run(
        first_kernel, "first", 7, [alive_in, *per_clip(clips_in), *quad_reduce],
        [*per_clip(shaped(tall)), *whole(narrow_note)],
        [*vector_scratch, pltpu.VMEM((D, MID), bf16), dma(16)], clips,
    )
    got = exchange(jnp.concatenate([note, early], axis=2))
    got, early = got[:, :, : MID // 4], got[:, :, MID // 4 :].reshape(devices, room)
    every_view = early[:, :clips]
    every_alive = (every_view < videos_all).astype(f32)
    counts = jnp.sum(every_alive, axis=1, keepdims=True) * FRAME_ROWS
    start = clips + own_videos * classes
    every_cotangent = early[:, clips:start].reshape(videos_all, classes)
    params = []
    for vector in vectors:
        params.append(early[::rep_count, start : start + vector.shape[0]].reshape(1, -1))
        start += vector.shape[0]
    g_one, s_one, g_two, s_two, g_three, s_three = params
    video_count = jnp.sum(
        (every_view.reshape(1, -1) == video_list.astype(f32)[:, None]).astype(f32), axis=1
    )
    every_share = every_cotangent / video_count[:, None]
    logit_grad = jnp.sum(members[:, :, None] * every_share[:, None, :], axis=0)
    logit_grad = jnp.pad(logit_grad.astype(bf16), ((0, 8 - clips), (0, 256 - classes)))
    stack_spatial, stack_wide = moves.stack(30, high, 576, 384)
    stack_spatial = moves.across_again(*moves.across_both(stack_spatial))
    norm_one, hidden, diff_even, diff_odd, summary = run(
        difference_kernel, "difference", 0.2,
        whole(got, counts, first, g_one, s_one, following, later),
        whole(shaped((2, MID)), in_grid, packed, packed, shaped((planes, MID))), [natural, field],
    )
    quad_diff = moves.complete(*stack_diff)
    gating, boost_even, boost_odd = run(
        gate_kernel, "gate", 0.2, [*whole(diff_even, diff_odd, summary, hidden), *quad_diff],
        whole(in_grid, packed, packed), [field, w_mid, w_small, dma(16), dma(16)],
    )
    quad_high = moves.complete_quarters(stack_spatial[0], *map(run.hold, stack_spatial[1:]))
    stack_wide = moves.across_both(run.hold(stack_wide))
    second, note = run(
        spatial_kernel, "spatial", 13, [alive_in, *whole(boost_even, boost_odd), *quad_high],
        whole(shaped(tall), narrow_note), [natural, field, w_mid, dma(32)],
    )
    got = exchange(note)
    quad_wide = moves.complete_quarters(*moves.across_again(*map(run.hold, stack_wide)))
    norm_two, hidden_two, third, note = run(
        expand_kernel, "expand", 9,
        [alive_in, *whole(got, counts), *per_clip(second), *whole(g_two, s_two), *quad_wide],
        [*whole(shaped((2, MID))), *per_clip(shaped(tall, bf16), shaped(tall_wide)), *whole(wide_note)],
        [w_wide, *[pltpu.VMEM((clips, 1, D), f32)] * 2, dma(128)], clips,
    )
    got = exchange(note)
    part = shaped((8, 144, 256), bf16)
    norm_three, normed, summed_grad, note, video_sums, grad_class, class_theirs, class_mine = run(
        outcome_kernel, "outcome", 17,
        [
            alive_in, *whole(got, counts), *per_clip(third, clips_in),
            *whole(g_three, s_three, logit_grad, members), *quad_wide,
        ],
        [
            *whole(shaped((2, D))), *per_clip(shaped(tall_wide, bf16), shaped(tall_wide, bf16)),
            *whole(wide_note, shaped((videos_all, 256)), shaped((D, 256), bf16), part, part),
        ],
        [
            pltpu.VMEM((D, 256), bf16), pltpu.VMEM((8, D), f32), pltpu.VMEM((2, D), f32),
            pltpu.VMEM((8, D), f32), pltpu.VMEM((2, D), f32), dma(64),
        ],
        clips,
    )
    got = exchange(note)
    expand_theirs, expand_mine, pre_two_grad, note, grads_three = run(
        third_kernel, "third", 18,
        [
            alive_in, *whole(got, counts), *per_clip(normed, summed_grad), *whole(g_three, norm_three),
            *per_clip(hidden_two, second), *whole(norm_two, g_two, s_two), *quad_wide,
        ],
        [
            *whole(shaped((MID, D // 2), bf16), shaped((MID, D // 2), bf16)), *per_clip(shaped(tall)),
            *whole(narrow_note, shaped((2, D))),
        ],
        [
            w_wide, pltpu.VMEM((MID, D), f32), pltpu.VMEM((2, MID), f32),
            pltpu.VMEM((FRAME_ROWS, D), bf16), pltpu.VMEM((3, D), f32), dma(128),
        ],
        clips,
    )
    got = exchange(note)
    from_core = lambda array: swap(array, CORE) if on_block else jnp.zeros_like(array)
    if on_block:
        half = shaped((4, 400, 256), bf16)
        expand_sent, expand_kept = run(
            expand_cut_kernel, "expand_cut", 3,
            whole(expand_mine, from_core(expand_theirs), class_mine, from_core(class_theirs)), whole(half, half),
        )
        expand_there = swap(expand_sent, Y)
    grads_two, low_even, low_odd, *spatial_theirs, offset = run(
        second_kernel, "second", 10,
        [alive_in, *whole(got, counts, pre_two_grad, second, norm_two, g_two, g_one, s_one, boost_even, boost_odd)],
        whole(
            shaped((2, MID)), packed, packed, *[shaped((3 * MID, MID // 2), bf16)] * 3, shaped((MID, MID))
        ),
        [natural, field],
    )
    spatial_there = [from_core(part) for part in spatial_theirs]
    if on_block:
        expand_group = moves.fold(expand_kept, expand_there)
    narrow = shaped((9 * MID, 128), bf16)
    spatial_sent, spatial_kept = run(
        own_spatial_kernel, "own_spatial", 9, whole(boost_even, boost_odd, low_even, offset, *spatial_there),
        whole(narrow, narrow), [pltpu.VMEM((MID, MID // 2), bf16)],
    )
    if on_block:
        spatial_there = swap(spatial_sent, X)
    hidden_grad, gate_even, gate_odd, pooled_theirs, pooled_mine, summary_grad = run(
        boost_back_kernel, "boost_back", 18,
        [*whole(low_even, low_odd, hidden, gating, summary), *quad_high, *quad_diff],
        whole(
            in_grid, packed, packed, shaped((MID, MID // 2), bf16), shaped((MID, MID // 2), bf16),
            shaped((planes, MID)),
        ),
        [field, w_mid, w_small, dma(32), dma(16)],
    )
    diff_theirs = run(
        their_diff_kernel, "their_diff", 8, whole(diff_even, diff_odd, gate_even, pooled_theirs),
        whole(*[shaped((taps * MID, MID // 2), bf16) for taps in (4, 4, 2)]),
    )
    diff_there = [from_core(part) for part in diff_theirs]
    if on_block:
        expand_group = [moves.totals(expand_group)]
        spatial_sent, spatial_kept = moves.by_y(spatial_kept, [spatial_there], 576)
        spatial_there = swap(spatial_sent, Y)
    narrow = shaped((10 * MID, 128), bf16)
    diff_sent, diff_kept = run(
        own_diff_kernel, "own_diff", 9, whole(diff_even, diff_odd, gate_even, pooled_mine, *diff_there),
        whole(narrow, narrow), [pltpu.VMEM((MID, MID // 2), bf16)],
    )
    if on_block:
        diff_there = swap(diff_sent, X)
    pre_one_grad, note = run(
        diff_back_kernel, "diff_back", 17,
        [
            alive_in, *whole(gate_even, gate_odd, summary_grad, hidden_grad, first, norm_one, g_one, s_one),
            *whole(before, earlier, later), *quad_diff,
        ],
        whole(shaped(tall), narrow_note), [natural, field, w_mid, dma(16)],
    )
    got = exchange(note)
    if on_block:
        spatial_group = moves.fold(spatial_kept, spatial_there)
        diff_sent, diff_kept = moves.by_y(diff_kept, [diff_there], 576, 64)
        diff_there = swap(diff_sent, Y)
    grads_one, low, *reduce_theirs, reduce_mine = run(
        reduce_kernel, "reduce", 9,
        [
            alive_in, *whole(got, counts), *per_clip(pre_one_grad, first), *whole(norm_one, g_one),
            *per_clip(clips_in),
        ],
        [
            *whole(shaped((2, MID))), *per_clip(shaped(tall, bf16)),
            *whole(*[shaped((D // 2, MID // 2), bf16)] * 2, shaped((D, MID // 2), bf16)),
        ],
        [pltpu.VMEM((D, MID), f32)], clips,
    )
    reduce_there = [from_core(part) for part in reduce_theirs]
    if on_block:
        spatial_group = [moves.totals(spatial_group)]
        diff_group = moves.fold(diff_kept, diff_there)
        reduce_sent, reduce_kept = moves.by_y(reduce_mine, reduce_there, 256)
        reduce_there = swap(reduce_sent, Y)
    (clips_grad,) = run(
        input_kernel, "input", 9, [*per_clip(low), *quad_reduce, *per_clip(summed_grad)],
        per_clip(shaped(tall_wide, bf16)), [pltpu.VMEM((D, MID), bf16), dma(16)], clips,
    )

    if on_block:
        total = moves.totals(expand_group, diff_group, spatial_group)
        reduce_group = moves.fold(reduce_kept, reduce_there)
        rest = moves.totals(reduce_group)
        rest_there = swap(rest, X)
        (total,) = run(
            meet_kernel, "meet", 2, whole(total, swap(total, X)), whole(shaped((1616, 256), bf16))
        )
        shapes = ((64, D), (256, 256), (16, 256), (576, MID), (64, MID), (576, MID))
        out_expand, out_class, videos, out_diff, out_pooled, out_spatial = run(
            finish_kernel, "finish", 3, whole(total, swap(total, CORE)), whole(*map(shaped, shapes))
        )
        video_total = lax.dynamic_slice_in_dim(videos, lax.axis_index("rep") // 2, 1)
        total = (rest.astype(f32) + rest_there.astype(f32)).astype(bf16)
        (out_reduce,) = run(
            join_kernel, "join", 2, whole(total, swap(total, CORE)), whole(shaped((256, MID)))
        )
    else:
        out_spatial = moves.scatter(moves.both_x(spatial_sent, spatial_kept), jnp.concatenate(spatial_theirs))
        out_expand = moves.scatter(expand_mine, expand_theirs)
        half, diff_theirs = moves.both_x(diff_sent, diff_kept), jnp.concatenate(diff_theirs)
        out_diff = moves.scatter(half[: 9 * MID], diff_theirs[: 9 * MID])
        out_pooled = moves.scatter(half[9 * MID :], diff_theirs[9 * MID :])
        out_reduce = moves.scatter(reduce_mine, jnp.concatenate(reduce_theirs))
        out_class = moves.scatter_rows(grad_class)
        video_total = lax.psum_scatter(video_sums, EVERY, scatter_dimension=0, tiled=True)
    place = lax.axis_index("fsdp") * rep_count + lax.axis_index("rep")
    own_counts = lax.dynamic_slice_in_dim(video_count, place * own_videos, own_videos)
    video_logits = video_total[:, :classes] / own_counts[:, None]

    def own_piece(grads, row):
        length = grads.shape[1] // fsdp_count
        return lax.dynamic_slice(grads, (row, lax.axis_index("fsdp") * length), (1, length))[0]

    return (
        video_logits,
        clips_grad,
        out_reduce,
        own_piece(grads_one, 1),
        own_piece(grads_one, 0),
        out_diff,
        out_pooled,
        out_spatial,
        own_piece(grads_two, 1),
        own_piece(grads_two, 0),
        out_expand,
        own_piece(grads_three, 1),
        own_piece(grads_three, 0),
        out_class[:, :classes],
    )


def solution(mesh):
    clips, weight, vector = P(EVERY, None, None), P("fsdp", None), P("fsdp")
    rows = P(EVERY, None)
    placed = (
        clips, P(EVERY), rows,
        weight, vector, vector,
        weight, weight, weight, vector, vector,
        weight, vector, vector,
        weight, rows,
    )
    return jax.shard_map(
        local,
        mesh=mesh,
        in_specs=placed,
        out_specs=(
            rows, clips,
            weight, vector, vector,
            weight, weight, weight, vector, vector,
            weight, vector, vector,
            weight,
        ),
        check_vma=False,
    )
```

```python
import functools

import jax
import jax.numpy as jnp
from jax import lax
from jax.experimental import pallas as pl
from jax.experimental.pallas import tpu as pltpu
from jax.sharding import PartitionSpec as P

D = 2048
MID = 512
EVERY = ("fsdp", "rep")

epsilon = 1e-05
f32 = jnp.float32
bf16 = jnp.bfloat16

SEGS = 8
SIDE = 7
PIXELS = SIDE * SIDE
FRAME_ROWS = SEGS * PIXELS
WIDE = SIDE + 1
VMEM_LIMIT = 58 * 2**20
SCALE = 2.0


class Grid:
    def __init__(self, clips):
        self.clips = clips
        self.planes = clips * SEGS
        self.rows = SIDE * WIDE * self.planes
        self.lead = -(-((WIDE + 1) * self.planes) // 16) * 16
        self.total = self.rows + 2 * self.lead
        self.offsets = [
            (WIDE * dy + dx) * self.planes for dy in (-1, 0, 1) for dx in (-1, 0, 1)
        ]

    @classmethod
    def of(cls, total):
        clips = 1
        while cls(clips).total < total:
            clips += 1
        return cls(clips)

    def tap(self, even, odd, tap, start, count):
        offset = self.offsets[tap]
        if offset % 16 == 0:
            return even[pl.ds(self.lead + start + offset, count), :]
        return odd[pl.ds(self.lead + start + offset - 8, count), :]

    def clear_edges(self, field):
        zeros = jnp.zeros((self.lead, MID), f32)
        field[pl.ds(0, self.lead), :] = zeros
        field[pl.ds(self.lead + self.rows, self.lead), :] = zeros
        field[pl.ds(self.total, 8), :] = zeros[:8]

    def pack(self, field, even, odd):
        step = self.total // 7

        @pl.loop(0, 7)
        def _(i):
            start = pl.multiple_of(i * step, 16)
            even[pl.ds(start, step), :] = field[pl.ds(start, step), :].astype(bf16)
            odd[pl.ds(start, step), :] = field[pl.ds(start + 8, step), :].astype(bf16)


def sigmoid(values):
    return 0.5 * jnp.tanh(0.5 * values) + 0.5


def quarters(ref, rows=slice(None)):
    return jnp.concatenate([ref[block, rows, :] for block in range(4)], axis=1)


def put_quarters(ref, rows, value):
    for block in range(4):
        ref[block, rows, :] = value[:, block * 128 : (block + 1) * 128]


def clip_pixel(clip, pixel):
    return pl.ds(clip * FRAME_ROWS + pixel, SEGS, stride=PIXELS)


def send_out(payload, low, high):
    count, _, lanes = payload.shape
    for row in range(4):
        for at, vector in ((row, low), (row + 4, high)):
            payload[:, at, :] = jnp.broadcast_to(
                vector[:, row * lanes : (row + 1) * lanes], (count, lanes)
            )


def received(got, at):
    return jnp.concatenate([got[:, row, :] for row in range(at, at + 4)], axis=1)


def joint_moments(got, counts):
    count = counts[...]
    population = jnp.sum(count, axis=0, keepdims=True)
    means, squares = received(got, 0), received(got, 4)
    center = jnp.sum(count * means, axis=0, keepdims=True) / population
    offset = means - center
    spread = jnp.sum(squares + count * offset * offset, axis=0, keepdims=True) / population
    return center, lax.rsqrt(spread + epsilon)


def own_moments(alive, means, squares):
    clips = len(means)
    alive_sum = sum(alive[clip] for clip in range(clips))
    mean = sum(alive[clip] * means[clip] for clip in range(clips)) / jnp.maximum(alive_sum, 1.0)
    square = 0.0
    for clip in range(clips):
        offset = means[clip] - mean
        square = square + alive[clip] * (squares[clip] + FRAME_ROWS * offset * offset)
    return mean, square


def clip_moments(values):
    mean = jnp.sum(values, axis=0, keepdims=True) * (1.0 / FRAME_ROWS)
    offset = values - mean
    return mean, jnp.sum(offset * offset, axis=0, keepdims=True)


def joint_sums(got, counts):
    population = jnp.sum(counts[...], axis=0, keepdims=True)
    total = jnp.sum(got[...], axis=0)
    low = jnp.concatenate([total[row : row + 1] for row in range(4)], axis=1)
    high = jnp.concatenate([total[row : row + 1] for row in range(4, 8)], axis=1)
    return low, high, low / population, high / population


def contract_rows(left, right):
    return lax.dot_general(left, right, (((0,), (0,)), ((), ())), preferred_element_type=f32)


def contract_lanes(left, right):
    return lax.dot_general(left, right, (((1,), (1,)), ((), ())), preferred_element_type=f32)


def dot(left, right):
    return jnp.dot(left, right, preferred_element_type=f32)


def first_kernel(at, alive, clips_in, *refs):
    quads, (first, payload, means, squares, weight, sems) = refs[:4], refs[4:]
    clip = pl.program_id(0)

    @pl.when(clip == 0)
    def _():
        wait_all(fetch(at, quads, 0, weight, sems))

    first[0] = dot(clips_in[0], weight[...])
    mean, square = clip_moments(first[0])
    means[clip] = mean
    squares[clip] = square

    @pl.when(clip == pl.num_programs(0) - 1)
    def _():
        count = means.shape[0]
        mean, square = own_moments(
            alive, [means[i] for i in range(count)], [squares[i] for i in range(count)]
        )
        send_out(payload, mean, square)


def difference_kernel(
    at, got, counts, first, gain, shift, following, later,
    norm, hidden, diff_even, diff_odd, summary, natural, field,
):
    grid = Grid(first.shape[0])
    center, scale = joint_moments(got, counts)
    norm[0:1] = center
    norm[1:2] = scale
    ratio = scale * gain[...]
    for clip in range(grid.clips):

        @pl.loop(0, SIDE)
        def _(part):
            rows = pl.ds(pl.multiple_of(part * 56, 8), 56)
            pre = (first[clip, rows, :] - center) * ratio + shift[...]
            value = pre * sigmoid(pre)
            put_quarters(natural, pl.ds(pl.multiple_of(clip * FRAME_ROWS + part * 56, 8), 56), value)

    grid.clear_edges(field)
    zeros = jnp.zeros((grid.planes, MID), f32)

    def spread_row(y, totals):
        base = pl.multiple_of(y * (WIDE * grid.planes), 8)
        totals = list(totals)
        for x in range(SIDE):
            for clip in range(grid.clips):
                place = base + x * grid.planes + clip * SEGS
                own = quarters(natural, clip_pixel(clip, y * SIDE + x))
                index = following[pl.ds(clip * SEGS, SEGS), :]
                after = jnp.concatenate(
                    [
                        jnp.take_along_axis(own[:, b * 128 : (b + 1) * 128], index, axis=0)
                        for b in range(4)
                    ],
                    axis=1,
                )
                step = (after - own) * later[pl.ds(clip * SEGS, SEGS), 0:1]
                step = step.astype(bf16).astype(f32)
                hidden[pl.ds(place, SEGS), :] = own
                field[pl.ds(grid.lead + place, SEGS), :] = step
                totals[clip] = totals[clip] + step
        edge = base + SIDE * grid.planes
        hidden[pl.ds(edge, grid.planes), :] = zeros
        field[pl.ds(grid.lead + edge, grid.planes), :] = zeros
        return tuple(totals)

    totals = lax.fori_loop(0, SIDE, spread_row, (zeros[:SEGS],) * grid.clips)
    mean = (jnp.concatenate(totals, axis=0) * (1.0 / PIXELS)).astype(bf16)
    summary[...] = mean.astype(f32)
    grid.pack(field, diff_even, diff_odd)


def gate_kernel(at, diff_even, diff_odd, summary, hidden, *refs):
    quads = refs[:4]
    gating, boost_even, boost_odd, field, weight, w_pooled, sems, more_sems = refs[4:]
    grid = Grid.of(diff_even.shape[0])
    copies = fetch(at, quads, 0, weight, sems) + fetch(at, quads, 576, w_pooled, more_sems)
    grid.clear_edges(field)
    wait_all(copies)
    pooled_term = dot(summary[...].astype(bf16), w_pooled[...])
    part = grid.rows // 2
    for start in (0, part):
        total = None
        for tap in range(9):
            term = dot(grid.tap(diff_even, diff_odd, tap, start, part), weight[pl.ds(tap * MID, MID), :])
            total = term if total is None else total + term
        gating[pl.ds(start, part), :] = total

    def boost(pixel):
        rows = pl.ds(pl.multiple_of(pixel * grid.planes, 8), grid.planes)
        gate = sigmoid(gating[rows, :] + pooled_term)
        gating[rows, :] = gate
        value = hidden[rows, :] * (1.0 + gate)
        field[pl.ds(pl.multiple_of(grid.lead + pixel * grid.planes, 8), grid.planes), :] = value

    pl.loop(0, SIDE * WIDE)(boost)
    grid.pack(field, boost_even, boost_odd)


def spatial_kernel(at, alive, boost_even, boost_odd, *refs):
    quads, (second, payload, natural, field, w_spatial, sems) = refs[:8], refs[8:]
    grid = Grid(second.shape[0])
    wait_all(fetch(at, quads, 0, w_spatial, sems))
    part = grid.rows // 2
    for start in (0, part):
        total = None
        for tap in range(9):
            term = dot(grid.tap(boost_even, boost_odd, tap, start, part), w_spatial[pl.ds(tap * MID, MID), :])
            total = term if total is None else total + term
        field[pl.ds(start, part), :] = total
    to_natural(grid, lambda at, clip: field[pl.ds(at, SEGS), :], natural)
    means, squares = [], []
    for clip in range(grid.clips):
        second[clip] = quarters(natural, pl.ds(clip * FRAME_ROWS, FRAME_ROWS))
        mean, square = clip_moments(second[clip])
        means.append(mean)
        squares.append(square)
    mean, square = own_moments(alive, means, squares)
    send_out(payload, mean, square)


def to_natural(grid, tile, natural):
    @pl.loop(0, SIDE)
    def _(y):
        for x in range(SIDE):
            for clip in range(grid.clips):
                at = pl.multiple_of(y * (WIDE * grid.planes), 8) + x * grid.planes + clip * SEGS
                put_quarters(natural, clip_pixel(clip, y * SIDE + x), tile(at, clip))


def expand_kernel(
    at, alive, got, counts, second, gain, shift, *refs
):
    w_expand, norm, hidden, third, payload, means, squares = refs
    clip = pl.program_id(0)
    center, scale = joint_moments(got, counts)

    @pl.when(clip == 0)
    def _():
        norm[0:1] = center
        norm[1:2] = scale

    ratio = scale * gain[...]
    pre = (second[0] - center) * ratio + shift[...]
    hidden[0] = (pre * sigmoid(pre)).astype(bf16)
    third[0] = dot(hidden[0], w_expand[...])
    mean, square = clip_moments(third[0])
    means[clip] = mean
    squares[clip] = square

    @pl.when(clip == pl.num_programs(0) - 1)
    def _():
        count = means.shape[0]
        mean, square = own_moments(
            alive, [means[i] for i in range(count)], [squares[i] for i in range(count)]
        )
        send_out(payload, mean, square)


def outcome_kernel(
    at, alive, got, counts, third, clips_in, gain, shift, logit_grad, members, *refs
):
    w_class, norm, normed, summed_grad, payload, video_sums, grad_class, theirs, mine = refs[:9]
    pooled_grad, sums, pooled, moments = refs[9:]
    clip = pl.program_id(0)

    @pl.when(clip == 0)
    def _():
        center, scale = joint_moments(got, counts)
        norm[0:1] = center
        norm[1:2] = scale
        moments[0:1] = center
        moments[1:2] = scale
        pooled_grad[...] = contract_lanes(logit_grad[...], w_class[...]) * (1.0 / FRAME_ROWS)
        sums[...] = jnp.zeros_like(sums)
        pooled[...] = jnp.zeros_like(pooled)

    weight = alive[clip]
    for lane in range(0, D, 512):
        lanes = pl.ds(lane, 512)
        center, scale = moments[0:1, lanes], moments[1:2, lanes]
        g, s = gain[:, lanes], shift[:, lanes]
        slope_grad = pooled_grad[pl.ds(clip, 1), lanes]

        def piece(start, count, carry):
            rows = pl.ds(start, count)
            value = (third[0, rows, lanes] - center) * scale
            total = value * g + s + clips_in[0, rows, lanes].astype(f32)
            sigma = sigmoid(total)
            out = total * sigma
            grad = slope_grad * (sigma + out * (1.0 - sigma))
            normed[0, rows, lanes] = value.astype(bf16)
            summed_grad[0, rows, lanes] = grad.astype(bf16)
            eights = lambda v: jnp.sum(v.reshape(count // 8, 8, 512), axis=0)
            return (
                carry[0] + eights(grad),
                carry[1] + eights(grad * value),
                carry[2] + eights(out),
            )

        zero = jnp.zeros((8, 512), f32)
        carry = lax.fori_loop(
            0,
            FRAME_ROWS // 16,
            lambda i, c: piece(pl.multiple_of(i * 16, 16), 16, c),
            (zero,) * 3,
            unroll=4,
        )
        tail = FRAME_ROWS - FRAME_ROWS % 16
        if tail < FRAME_ROWS:
            carry = piece(tail, FRAME_ROWS - tail, carry)
        low, high, mean = (jnp.sum(v, axis=0, keepdims=True) for v in carry)
        sums[0:1, lanes] = sums[0:1, lanes] + weight * low
        sums[1:2, lanes] = sums[1:2, lanes] + weight * high
        pooled[pl.ds(clip, 1), lanes] = mean * (1.0 / FRAME_ROWS)

    @pl.when(clip == pl.num_programs(0) - 1)
    def _():
        send_out(payload, sums[0:1], sums[1:2])
        rounded = pooled[...].astype(bf16)
        logits = dot(rounded, w_class[...])
        total = 0.0
        for i in range(clips_of(members)):
            total = total + members[:, i : i + 1] * logits[i : i + 1]
        video_sums[...] = total
        grad_class[...] = contract_rows(rounded, logit_grad[...]).astype(bf16)
        for shard in range(8):
            for out, core in ((theirs, 1 - at[1]), (mine, at[1])):
                rows = pl.ds(pl.multiple_of(shard * 256 + core * 128, 128), 128)
                out[shard, 0:128, :] = grad_class[rows, :]
                videos = [video_sums[pl.ds(shard * 4 + x * 2 + core, 1), :] for x in (0, 1)]
                videos += [jnp.zeros((14, 256), f32)]
                out[shard, 128:144, :] = jnp.concatenate(videos).astype(bf16)


def clips_of(members):
    return members.shape[1]


def third_kernel(
    at, alive, got, counts, normed, summed_grad, gain, norm_three, hidden, second, norm_two, gain_two, shift_two,
    *refs,
):
    w_expand, theirs, mine, pre_grad, payload, grads, total, sums, low, columns = refs
    clip = pl.program_id(0)

    @pl.when(clip == 0)
    def _():
        total[...] = jnp.zeros_like(total)
        columns[...] = jnp.zeros_like(columns)
        sums[...] = jnp.zeros_like(sums)
        shift_grad, gain_grad, shift_share, gain_share = joint_sums(got, counts)
        grads[0:1] = shift_grad
        grads[1:2] = gain_grad
        columns[1:2] = shift_share
        columns[2:3] = gain_share

    weight = alive[clip]
    ratio = gain[...] * norm_three[1:2]
    for lane in range(0, D, 512):
        lanes = pl.ds(lane, 512)
        shift_share, gain_share = columns[1:2, lanes] * weight, columns[2:3, lanes] * weight
        r = ratio[:, lane : lane + 512]

        def piece(start, count, carry):
            rows = pl.ds(start, count)
            value = summed_grad[0, rows, lanes].astype(f32) - (
                shift_share + normed[0, rows, lanes].astype(f32) * gain_share
            )
            value = (r * value).astype(bf16)
            low[rows, lanes] = value
            return carry + jnp.sum(value.astype(f32).reshape(count // 8, 8, 512), axis=0)

        carry = lax.fori_loop(
            0,
            FRAME_ROWS // 16,
            lambda i, c: piece(pl.multiple_of(i * 16, 16), 16, c),
            jnp.zeros((8, 512), f32),
            unroll=4,
        )
        tail = FRAME_ROWS - FRAME_ROWS % 16
        if tail < FRAME_ROWS:
            carry = piece(tail, FRAME_ROWS - tail, carry)
        columns[0:1, lanes] = columns[0:1, lanes] + jnp.sum(carry, axis=0, keepdims=True)
    grad_out = low[pl.ds(0, FRAME_ROWS), :]
    total[...] = total[...] + contract_rows(hidden[0], grad_out)
    back = contract_lanes(grad_out, w_expand[...])
    value = (second[0] - norm_two[0:1]) * norm_two[1:2]
    pre = value * gain_two[...] + shift_two[...]
    sigma = sigmoid(pre)
    grad = back * (sigma * (1.0 + pre * (1.0 - sigma)))
    pre_grad[0] = grad
    sums[0:1] = sums[0:1] + weight * jnp.sum(grad, axis=0, keepdims=True)
    sums[1:2] = sums[1:2] + weight * jnp.sum(grad * value, axis=0, keepdims=True)

    @pl.when(clip == pl.num_programs(0) - 1)
    def _():
        send_out(payload, sums[0:1], sums[1:2])
        mean = usual_silu(shift_two[...], gain_two[...])
        offset = outer(mean, columns[0:1])
        total[...] = total[...] - offset
        core = at[1]
        theirs[...] = total[:, core_lanes(1 - core, D // 2)].astype(bf16)
        mine[...] = total[:, core_lanes(core, D // 2)].astype(bf16)


def usual_silu(shift, gain):
    silu = lambda v: v * sigmoid(v)
    wide = 3.0**0.5 * gain
    return (2.0 / 3.0) * silu(shift) + (silu(shift + wide) + silu(shift - wide)) * (1.0 / 6.0)


def outer(column, row):
    return jnp.swapaxes(jnp.broadcast_to(column, (8, column.shape[1])), 0, 1)[:, 0:1] * row


def to_grid(grid, natural, put):
    @pl.loop(0, SIDE)
    def _(y):
        base = pl.multiple_of(y * (WIDE * grid.planes), 8)
        for x in range(SIDE):
            for clip in range(grid.clips):
                put(base + x * grid.planes + clip * SEGS, clip, quarters(natural, clip_pixel(clip, y * SIDE + x)))
        put(base + SIDE * grid.planes, None, jnp.zeros((grid.planes, MID), f32))


def second_kernel(
    at, alive, got, counts, pre_grad, second, norm_two, gain_two, gain_one, shift_one, boost_even, boost_odd,
    grads, low_even, low_odd, theirs0, theirs1, theirs2, offset, natural, field,
):
    grid = Grid(pre_grad.shape[0])
    shift_grad, gain_grad, shift_share, gain_share = joint_sums(got, counts)
    grads[0:1] = shift_grad
    grads[1:2] = gain_grad
    center, scale = norm_two[0:1], norm_two[1:2]
    ratio = gain_two[...] * scale
    columns = jnp.zeros((8, MID), f32)
    for clip in range(grid.clips):
        weight = alive[clip]

        def piece(part, columns):
            rows = pl.ds(pl.multiple_of(part * 56, 8), 56)
            value = (second[clip, rows, :] - center) * scale
            grad = ratio * (pre_grad[clip, rows, :] - weight * (shift_share + value * gain_share))
            grad = grad.astype(bf16).astype(f32)
            put_quarters(natural, pl.ds(pl.multiple_of(clip * FRAME_ROWS + part * 56, 8), 56), grad)
            return columns + jnp.sum(grad.reshape(7, 8, MID), axis=0)

        columns = lax.fori_loop(0, SIDE, piece, columns)
    columns = jnp.sum(columns, axis=0, keepdims=True)
    grid.clear_edges(field)

    def put(at, clip, value):
        field[pl.ds(grid.lead + at, value.shape[0]), :] = value

    to_grid(grid, natural, put)
    grid.pack(field, low_even, low_odd)
    offset[...] = outer(1.5 * usual_silu(shift_one[...], gain_one[...]), columns)
    lanes = core_lanes(1 - at[1], MID // 2)
    grad_out = low_even[pl.ds(grid.lead, grid.rows), lanes]
    for tap in range(9):
        term = contract_rows(grid.tap(boost_even, boost_odd, tap, 0, grid.rows), grad_out)
        theirs = (theirs0, theirs1, theirs2)[tap // 3]
        theirs[pl.ds(tap % 3 * MID, MID), :] = (term - offset[:, lanes]).astype(bf16)


def own_spatial_kernel(
    at, boost_even, boost_odd, low_even, offset, there0, there1, there2, sent, kept, total
):
    grid = Grid.of(low_even.shape[0])
    lanes = core_lanes(at[1], MID // 2)
    grad_out = low_even[pl.ds(grid.lead, grid.rows), lanes]
    for tap in range(9):
        rows = pl.ds(tap * MID, MID)
        term = contract_rows(grid.tap(boost_even, boost_odd, tap, 0, grid.rows), grad_out)
        there = (there0, there1, there2)[tap // 3][pl.ds(tap % 3 * MID, MID), :]
        total[...] = (term - offset[:, lanes] + there.astype(f32)).astype(bf16)
        sent[rows, :] = total[:, core_lanes(1 - at[3], 128)]
        kept[rows, :] = total[:, core_lanes(at[3], 128)]


def boost_back_kernel(at, low_even, low_odd, hidden, gating, summary, *refs):
    spatial_quads, diff_quads = refs[:8], refs[8:12]
    hidden_grad, gate_even, gate_odd, pooled_theirs, pooled_mine, summary_grad = refs[12:18]
    field, w_spatial, w_pooled, sems, more_sems = refs[18:]
    copies = fetch(at, spatial_quads, 0, w_spatial, sems) + fetch(at, diff_quads, 576, w_pooled, more_sems)
    wait_all(copies)
    grid = Grid(hidden.shape[0] // (SIDE * WIDE * SEGS))
    part = grid.rows // 2
    for start in (0, part):
        total = None
        for tap in range(9):
            term = contract_lanes(
                grid.tap(low_even, low_odd, 8 - tap, start, part), w_spatial[pl.ds(tap * MID, MID), :]
            )
            total = term if total is None else total + term
        hidden_grad[pl.ds(start, part), :] = total
    grid.clear_edges(field)

    def piece(pixel, total):
        rows = pl.ds(pl.multiple_of(pixel * grid.planes, 8), grid.planes)
        grad, gate = hidden_grad[rows, :], gating[rows, :]
        hidden_grad[rows, :] = grad * (1.0 + gate)
        gate_grad = (grad * hidden[rows, :] * gate * (1.0 - gate)).astype(bf16).astype(f32)
        field[pl.ds(pl.multiple_of(grid.lead + pixel * grid.planes, 8), grid.planes), :] = gate_grad
        return total + gate_grad

    gate_sums = lax.fori_loop(0, SIDE * WIDE, piece, jnp.zeros((grid.planes, MID), f32))
    grid.pack(field, gate_even, gate_odd)
    high = gate_sums.astype(bf16)
    low = (gate_sums - high.astype(f32)).astype(bf16)
    mean = summary[...].astype(bf16)
    grad_pooled = contract_rows(mean, high) + contract_rows(mean, low)
    field[pl.ds(0, MID), :] = grad_pooled
    core = at[1]
    pooled_theirs[...] = field[pl.ds(0, MID), core_lanes(1 - core, MID // 2)].astype(bf16)
    pooled_mine[...] = field[pl.ds(0, MID), core_lanes(core, MID // 2)].astype(bf16)
    back = contract_lanes(high, w_pooled[...]) + contract_lanes(low, w_pooled[...])
    summary_grad[...] = back * (1.0 / PIXELS)


def their_diff_kernel(at, diff_even, diff_odd, gate_even, pooled, *theirs):
    grid = Grid.of(gate_even.shape[0])
    grad_out = gate_even[pl.ds(grid.lead, grid.rows), core_lanes(1 - at[1], MID // 2)]
    for tap in range(9):
        term = contract_rows(grid.tap(diff_even, diff_odd, tap, 0, grid.rows), grad_out)
        theirs[tap // 4][pl.ds(tap % 4 * MID, MID), :] = term.astype(bf16)
    theirs[2][pl.ds(MID, MID), :] = pooled[...]


def own_diff_kernel(
    at, diff_even, diff_odd, gate_even, pooled, there0, there1, there2, sent, kept, total
):
    grid = Grid.of(gate_even.shape[0])
    grad_out = gate_even[pl.ds(grid.lead, grid.rows), core_lanes(at[1], MID // 2)]
    for tap in range(10):
        rows = pl.ds(tap * MID, MID)
        if tap < 9:
            term = contract_rows(grid.tap(diff_even, diff_odd, tap, 0, grid.rows), grad_out)
        else:
            term = pooled[...].astype(f32)
        there = (there0, there1, there2)[tap // 4][pl.ds(tap % 4 * MID, MID), :]
        total[...] = (term + there.astype(f32)).astype(bf16)
        sent[rows, :] = total[:, core_lanes(1 - at[3], 128)]
        kept[rows, :] = total[:, core_lanes(at[3], 128)]


def diff_back_kernel(
    at, alive, gate_even, gate_odd, summary_grad, hidden_grad, first, norm_one, gain, shift, before, earlier, later,
    *refs,
):
    quads, (pre_grad, payload, natural, field, w_diff, sems) = refs[:4], refs[4:]
    grid = Grid(first.shape[0])
    wait_all(fetch(at, quads, 0, w_diff, sems))
    part = grid.rows // 2
    for start in (0, part):
        total = None
        for tap in range(9):
            term = contract_lanes(
                grid.tap(gate_even, gate_odd, 8 - tap, start, part), w_diff[pl.ds(tap * MID, MID), :]
            )
            total = term if total is None else total + term
        field[pl.ds(start, part), :] = total

    def tile(at, clip):
        planes = pl.ds(clip * SEGS, SEGS)
        grad = field[pl.ds(at, SEGS), :] + summary_grad[planes, :]
        index = before[planes, :]
        back = jnp.concatenate(
            [
                jnp.take_along_axis(grad[:, b * 128 : (b + 1) * 128], index, axis=0)
                for b in range(4)
            ],
            axis=1,
        )
        own = hidden_grad[pl.ds(at, SEGS), :]
        return own + back * earlier[planes, 0:1] - grad * later[planes, 0:1]

    to_natural(grid, tile, natural)
    center, scale = norm_one[0:1], norm_one[1:2]
    low = jnp.zeros((8, MID), f32)
    high = jnp.zeros((8, MID), f32)
    for clip in range(grid.clips):
        weight = alive[clip]

        def piece(step, carry):
            rows = pl.ds(pl.multiple_of(step * 56, 8), 56)
            value = (first[clip, rows, :] - center) * scale
            pre = value * gain[...] + shift[...]
            sigma = sigmoid(pre)
            grad = quarters(natural, pl.ds(pl.multiple_of(clip * FRAME_ROWS + step * 56, 8), 56))
            grad = grad * (sigma * (1.0 + pre * (1.0 - sigma)))
            pre_grad[clip, rows, :] = grad
            eights = lambda v: jnp.sum(v.reshape(7, 8, MID), axis=0) * weight
            return carry[0] + eights(grad), carry[1] + eights(grad * value)

        low, high = lax.fori_loop(0, SIDE, piece, (low, high))
    send_out(payload, jnp.sum(low, axis=0, keepdims=True), jnp.sum(high, axis=0, keepdims=True))


def reduce_kernel(
    at, alive, got, counts, pre_grad, first, norm_one, gain, clips_in,
    grads, low, theirs0, theirs1, mine, total,
):
    clip = pl.program_id(0)
    shift_grad, gain_grad, shift_share, gain_share = joint_sums(got, counts)

    @pl.when(clip == 0)
    def _():
        total[...] = jnp.zeros_like(total)
        grads[0:1] = shift_grad
        grads[1:2] = gain_grad

    center, scale = norm_one[0:1], norm_one[1:2]
    value = (first[0] - center) * scale
    grad = pre_grad[0] - alive[clip] * (shift_share + value * gain_share)
    low[0] = (gain[...] * scale * grad).astype(bf16)
    total[...] = total[...] + contract_rows(clips_in[0], low[0])

    @pl.when(clip == pl.num_programs(0) - 1)
    def _():
        core = at[1]
        lanes = core_lanes(1 - core, MID // 2)
        theirs0[...] = total[pl.ds(0, D // 2), lanes].astype(bf16)
        theirs1[...] = total[pl.ds(D // 2, D // 2), lanes].astype(bf16)
        mine[...] = total[:, core_lanes(core, MID // 2)].astype(bf16)


def input_kernel(at, low, *refs):
    quads, (summed_grad, clips_grad, weight, sems) = refs[:4], refs[4:]

    @pl.when(pl.program_id(0) == 0)
    def _():
        wait_all(fetch(at, quads, 0, weight, sems))

    back = contract_lanes(low[0], weight[...])
    clips_grad[0] = (back + summed_grad[0].astype(f32)).astype(bf16)


def cut_kernel(
    at, reduce_weight, diff_weight, pooled_weight, spatial_weight, expand_weight, class_weight,
    low, middle, high, wide,
):
    core = at[1]
    lanes = core_lanes(core, MID // 2)
    low[...] = reduce_weight[:, lanes]
    middle[0:576, :] = diff_weight[:, lanes]
    middle[576:640, :] = pooled_weight[:, lanes]
    high[...] = spatial_weight[:, pl.ds(pl.multiple_of(core * 256 + at[3] * 128, 128), 128)]
    for block in range(4):
        place = pl.ds(pl.multiple_of(core * 1024 + block * 256, 256), 256)
        wide[64 * block : 64 * (block + 1), :] = expand_weight[:, place]
    wide[256:384, :] = class_weight[pl.ds(pl.multiple_of(core * 128, 128), 128), :]


def stack_kernel(at, *refs):
    pieces, outs = refs[:4], refs[4:]
    start = 0
    for out in outs:
        rows = out.shape[1]
        for hop in range(4):
            out[jnp.bitwise_xor(at[2], hop)] = pieces[hop][pl.ds(start, rows), :]
        start += rows


def expand_cut_kernel(at, expand_mine, expand_there, class_mine, class_there, sent, kept):
    for z in range(4):
        for out, row in ((sent, 1 - at[0]), (kept, at[0])):
            shard = z * 2 + row
            rows = pl.ds(pl.multiple_of(shard * 64, 64), 64)
            value = expand_mine[rows, :].astype(f32) + expand_there[rows, :].astype(f32)
            for block in range(4):
                out[z, 64 * block : 64 * (block + 1), :] = value[
                    :, 256 * block : 256 * (block + 1)
                ].astype(bf16)
            value = class_mine[shard].astype(f32) + class_there[shard].astype(f32)
            out[z, 256:400, :] = value.astype(bf16)


def totals_kernel(counts, at, *refs):
    out, index, start = refs[-1], 0, 0
    for count in counts:
        value = sum(ref[...].astype(f32) for ref in refs[index : index + count])
        rows, lanes = value.shape
        if lanes == 128:
            rows //= 2
            value = jnp.concatenate([value[:rows], value[rows:]], axis=1)
        out[pl.ds(start, rows), :] = value.astype(bf16)
        index, start = index + count, start + rows


def meet_kernel(at, total, there, out):
    mine, other = total[0:400, :].astype(f32), there[0:400, :].astype(f32)
    out[0:400, :] = (mine + other).astype(bf16)
    start, place = 400, 400
    for rows in (320, 288):
        for ref, x in ((total, at[3]), (there, 1 - at[3])):
            for part in (0, 1):
                out[pl.ds(place + rows * part, rows), core_lanes(x, 128)] = ref[
                    pl.ds(start, rows), 128 * part : 128 * (part + 1)
                ]
        start, place = start + rows, place + 2 * rows


def finish_kernel(
    at, total, there, own_count, grad_expand, grad_class, videos, grad_diff, grad_pooled, grad_spatial
):
    for array, core in ((total, at[1]), (there, 1 - at[1])):
        for block in range(4):
            place = pl.ds(pl.multiple_of(core * 1024 + block * 256, 256), 256)
            grad_expand[:, place] = array[64 * block : 64 * (block + 1), :].astype(f32)
        value = array[256:384, :].astype(f32)
        grad_class[pl.ds(pl.multiple_of(core * 128, 128), 128), :] = value[:, : grad_class.shape[1]]
        place = core_lanes(core, 256)
        grad_diff[:, place] = array[400:976, :].astype(f32)
        grad_pooled[:, place] = array[976:1040, :].astype(f32)
        grad_spatial[:, place] = array[1040:1616, :].astype(f32)
    rows = total[384:400, : videos.shape[1]].astype(f32)
    videos[...] = jnp.where(at[3] == 0, rows[0:1], rows[1:2]) / own_count[...]


def fold_kernel(at, kept, there, own, *sent):
    for hop, out in enumerate((own, *sent)):
        z = jnp.bitwise_xor(at[2], hop)
        out[...] = (kept[z].astype(f32) + there[z].astype(f32)).astype(bf16)


def core_lanes(core, width):
    return pl.ds(pl.multiple_of(core * width, width), width)


def fetch(at, quads, start, weight, sems):
    count = weight.shape[0] // 8
    jobs = []
    for quad, shard, core, x in quad_places(at, quads):
        rows = pl.ds(pl.multiple_of(shard * count, 16), count)
        width = quad.shape[1]
        lanes = pl.ds(pl.multiple_of(core * 256 + x * 128, width), width)
        jobs.append((quad.at[pl.ds(start, count), :], weight.at[rows, lanes]))
    return start_all(jobs, sems)


def quad_places(at, quads):
    half = len(quads) // 2
    for index, quad in enumerate(quads):
        row = at[0] if index % 2 == 0 else 1 - at[0]
        core = at[1] if index < half else 1 - at[1]
        x = 0
        if half == 4:
            x = at[3] if index % 4 < 2 else 1 - at[3]
        for z in range(4):
            yield quad.at[z], z * 2 + row, core, x


def wide_kernel(at, *refs):
    quads, (w_expand, w_class) = refs[:4], refs[4:]
    for quad, shard, core, _ in quad_places(at, quads):
        rows = pl.ds(pl.multiple_of(shard * 64, 64), 64)
        for block in range(4):
            place = pl.ds(pl.multiple_of(core * 1024 + block * 256, 256), 256)
            w_expand[rows, place] = quad[pl.ds(64 * block, 64), :]
        rows = pl.ds(pl.multiple_of(shard * 256 + core * 128, 128), 128)
        w_class[rows, :] = quad[pl.ds(256, 128), :]


def start_all(jobs, sems):
    copies = [pltpu.make_async_copy(*job, sems.at[i]) for i, job in enumerate(jobs)]
    for copy in copies:
        copy.start()
    return copies


def wait_all(copies):
    for copy in copies:
        copy.wait()


def split_kernel(sizes, at, mine, *refs):
    theres, (sent, kept) = refs[:-2], refs[-2:]
    for z in range(4):
        there = theres[z * len(theres) // 4]
        for out, row in ((sent, 1 - at[0]), (kept, at[0])):
            start = place = 0
            for size in sizes:
                rows = pl.ds(pl.multiple_of(start + (z * 2 + row) * size, 16), size)
                first = z * len(theres) // 4 * mine.shape[0] // len(theres)
                there_rows = pl.ds(pl.multiple_of(start + (z * 2 + row) * size - first, 16), size)
                value = mine[rows, :].astype(f32) + there[there_rows, :].astype(f32)
                out[z, pl.ds(place, size), :] = value.astype(bf16)
                start, place = start + 8 * size, place + size


def join_kernel(at, mine, there, *outs):
    start = 0
    for out in outs:
        rows, lanes = out.shape
        for block in range(lanes // 512):
            for array, core in ((mine, at[1]), (there, 1 - at[1])):
                place = pl.ds(pl.multiple_of(core * (lanes // 2) + block * 256, 256), 256)
                out[:, place] = array[pl.ds(start + block * rows, rows), :].astype(f32)
        start += rows * (lanes // 512)


SCALARS = pl.BlockSpec(memory_space=pltpu.SMEM)
WHOLE = pl.BlockSpec(memory_space=pltpu.VMEM)


def each_clip(shape):
    return pl.BlockSpec((1, *shape[1:]), lambda clip: (clip, 0, 0))


def shaped(shape, dtype=f32):
    return jax.ShapeDtypeStruct(tuple(shape), dtype)


def whole(*arrays):
    return [(array, WHOLE) for array in arrays]


def anywhere(*arrays):
    return [(array, pl.BlockSpec(memory_space=pl.ANY)) for array in arrays]


def per_clip(*arrays):
    return [(array, each_clip(array.shape)) for array in arrays]


def dma(count):
    return pltpu.SemaphoreType.DMA((count,))


class Chain:
    def __init__(self, place):
        self.at = jnp.stack([jnp.asarray(part, jnp.int32) for part in place])
        self.factor = SCALE

    def __call__(self, kernel, name, micros, ins, outs, scratch=(), clips=None, after=()):
        skip = 1 + len(after)
        last = skip + len(ins) + len(outs)

        def body(*refs):
            for index in range(4):
                refs[last][index] = refs[0][index]
            kernel(refs[0], *refs[skip:last], *refs[last + 1 :])

        results = pl.pallas_call(
            body,
            out_shape=[*[shape for shape, _ in outs], shaped((4,), jnp.int32)],
            grid=(clips,) if clips else (),
            in_specs=[SCALARS, *[spec for _, spec in anywhere(*after)], *[spec for _, spec in ins]],
            out_specs=[*[spec for _, spec in outs], SCALARS],
            scratch_shapes=list(scratch),
            compiler_params=pltpu.CompilerParams(vmem_limit_bytes=VMEM_LIMIT),
            cost_estimate=pl.CostEstimate(
                flops=int(micros * self.factor * 1.1e9),
                bytes_accessed=int(micros * self.factor * 3.6e6),
                transcendentals=0,
            ),
            name=name,
        )(self.at, *after, *[array for array, _ in ins])
        self.at = results[-1]
        return results[:-1]

    def hold(self, array):
        return lax.optimization_barrier((array, self.at))[0]


def exchange(payload):
    return lax.all_to_all(payload, EVERY, 0, 0, tiled=True)


def swap(array, bit):
    count = lax.axis_size("fsdp") * lax.axis_size("rep")
    return lax.ppermute(array, EVERY, [(place, place ^ bit) for place in range(count)])


CORE, X, Y, Z = 1, 2, 4, 8


class Block:
    def __init__(self):
        place = lax.axis_index("fsdp") * 4 + lax.axis_index("rep")
        self.run = Chain([(place >> 2) & 1, place & 1, place >> 3, (place >> 1) & 1])

    def cut(self, *shards):
        sizes = ((256, 256), (640, 256), (576, 128), (384, 256))
        return self.run(cut_kernel, "cut", 3, whole(*shards), whole(*[shaped(size, bf16) for size in sizes]))

    def along_z(self, piece):
        return (piece, *[swap(piece, hop * Z) for hop in (1, 2, 3)])

    def stack(self, micros, pieces, *sizes, after=()):
        rows, lanes = pieces[0].shape
        shapes = [shaped((4, size, lanes), bf16) for size in sizes or (rows,)]
        return self.run(stack_kernel, "stack", micros, whole(*pieces), whole(*shapes), after=after)

    def across(self, own):
        return own, swap(own, Y)

    def complete(self, own, across):
        return anywhere(own, across, swap(own, CORE), swap(across, CORE))

    def complete_quarters(self, *mine):
        return anywhere(*mine, *[swap(part, CORE) for part in mine])

    def across_both(self, own):
        return own, swap(own, Y), swap(own, X)

    def across_again(self, own, across, over_x):
        return own, across, over_x, swap(across, X)

    def by_y(self, mine, theres, *sizes):
        half = shaped((4, sum(sizes), mine.shape[1]), bf16)
        kernel = functools.partial(split_kernel, sizes)
        return self.run(kernel, "split", 3, whole(mine, *theres), whole(half, half))

    def fold(self, kept, there):
        rows = shaped(kept.shape[1:], bf16)
        own, *others = self.run(fold_kernel, "fold", 3, whole(kept, there), whole(rows, rows, rows, rows))
        return own, *[swap(other, hop * Z) for hop, other in zip((1, 2, 3), others)]

    def totals(self, *groups):
        refs = [ref for group in groups for ref in group]
        rows = sum(group[0].shape[0] * group[0].shape[1] // 256 for group in groups)
        kernel = functools.partial(totals_kernel, [len(group) for group in groups])
        return self.run(kernel, "totals", 2, whole(*refs), whole(shaped((rows, 256), bf16)))[0]


class Anywhere:
    def __init__(self):
        self.run = Chain([0, 0, 0, 0])

    def cut(self, *shards):
        reduce_weight, diff, pooled, spatial, expand, classes = [
            lax.all_gather(shard, "fsdp", axis=0, tiled=True) for shard in shards
        ]
        low, diff, pooled, high = [
            array.reshape(4, 2, -1, 2, 256) for array in (reduce_weight, diff, pooled, spatial)
        ]
        middle = jnp.concatenate([diff, pooled], axis=2)
        high = high.reshape(4, 2, 576, 2, 2, 128)
        expand = jnp.moveaxis(expand.reshape(4, 2, 64, 2, 4, 256), 4, 2).reshape(4, 2, 256, 2, 256)
        classes = jnp.moveaxis(classes.reshape(4, 2, 2, 128, 256), 2, 3)
        return low, middle, high, jnp.concatenate([expand, classes], axis=2)

    def along_z(self, piece):
        return piece

    def stack(self, micros, piece, *sizes, after=()):
        cuts = [sum(sizes[:count]) for count in range(1, len(sizes))]
        return jnp.split(piece, cuts, axis=2)

    def across(self, piece):
        return (piece,)

    def across_both(self, piece):
        return (piece,)

    def across_again(self, piece):
        return (piece,)

    def complete(self, piece):
        return anywhere(*[piece[:, y, :, core] for core in (0, 1) for y in (0, 1)])

    def complete_quarters(self, piece):
        return anywhere(
            *[piece[:, y, :, core, x] for core in (0, 1) for x in (0, 1) for y in (0, 1)]
        )

    def scatter(self, lower, upper):
        grads = jnp.concatenate([lower, upper], axis=1)
        return self.scatter_rows(grads)

    def scatter_rows(self, grads):
        grads = grads.astype(f32)
        return lax.psum(lax.psum_scatter(grads, "fsdp", scatter_dimension=0, tiled=True), "rep")

    def both_x(self, sent, kept):
        return jnp.concatenate([kept, sent], axis=1)


def local(
    clips_in,
    view_ids,
    seg_order,
    reduce_weight,
    gain1,
    shift1,
    diff_weight,
    pooled_weight,
    spatial_weight,
    gain2,
    shift2,
    expand_weight,
    gain3,
    shift3,
    class_weight,
    video_cotangent,
):
    fsdp_count = lax.axis_size("fsdp")
    rep_count = lax.axis_size("rep")
    devices = fsdp_count * rep_count
    clips = clips_in.shape[0]
    own_videos, classes = video_cotangent.shape
    videos_all = own_videos * devices
    on_block = (fsdp_count, rep_count) == (8, 4)
    grid = Grid(clips)
    planes = grid.planes

    vectors = (gain1, shift1, gain2, shift2, gain3, shift3)
    early = [view_ids.astype(f32), video_cotangent.reshape(-1)]
    early += [vector.astype(f32) for vector in vectors]
    early = jnp.concatenate(early)
    room = -(-early.shape[0] // 1024) * 1024
    early = jnp.pad(early, (0, room - early.shape[0])).reshape(1, 8, room // 8)
    early = jnp.broadcast_to(early, (devices, 8, room // 8))

    moves = Block() if on_block else Anywhere()
    run = moves.run
    wide_class = jnp.pad(class_weight, ((0, 0), (0, 256 - classes)))
    pieces = moves.cut(
        reduce_weight, diff_weight, pooled_weight, spatial_weight, expand_weight, wide_class
    )

    alive = (view_ids < videos_all).astype(f32)
    video_list = jnp.arange(videos_all, dtype=jnp.int32)
    members = (video_list[:, None] == view_ids[None, :]).astype(f32)

    stations = jnp.arange(SEGS, dtype=jnp.int32)
    places = (seg_order[:, :, None] == stations).astype(jnp.int32)
    place = jnp.sum(places * stations[None, :, None], axis=1)
    is_last, is_first = place == SEGS - 1, place == 0
    at = lambda wanted: jnp.sum(
        (jnp.clip(wanted, 0, SEGS - 1)[:, :, None] == stations).astype(jnp.int32)
        * seg_order[:, None, :],
        axis=2,
    )
    lanes = lambda array: jnp.broadcast_to(array.reshape(planes, 1), (planes, 128))
    following = lanes(at(place + 1))
    before = lanes(at(place - 1))
    later = lanes(1.0 - is_last.astype(f32))
    earlier = lanes(1.0 - is_first.astype(f32))

    low, middle = moves.along_z(pieces[0]), moves.along_z(pieces[1])
    stack_reduce = moves.across(*moves.stack(2, low))
    stack_diff = moves.across(*moves.stack(30, middle))
    high = moves.along_z(run.hold(pieces[2]))
    quad_reduce = moves.complete(*stack_reduce)

    tall = (clips, FRAME_ROWS, MID)
    tall_wide = (clips, FRAME_ROWS, D)
    narrow_note = shaped((devices, 8, MID // 4))
    wide_note = shaped((devices, 8, D // 4))
    packed = shaped((grid.total, MID), bf16)
    in_grid = shaped((grid.rows, MID))
    natural = pltpu.VMEM((4, clips * FRAME_ROWS, 128), f32)
    field = pltpu.VMEM((grid.total + 8, MID), f32)
    alive_in = (alive, SCALARS)
    vector_scratch = [pltpu.VMEM((clips, 1, MID), f32)] * 2

    w_mid = pltpu.VMEM((9 * MID, MID), bf16)
    w_small = pltpu.VMEM((MID, MID), bf16)

    first, note = run(
        first_kernel, "first", 7, [alive_in, *per_clip(clips_in), *quad_reduce],
        [*per_clip(shaped(tall)), *whole(narrow_note)],
        [*vector_scratch, pltpu.VMEM((D, MID), bf16), dma(16)], clips,
    )
    got = exchange(jnp.concatenate([note, early], axis=2))
    got, early = got[:, :, : MID // 4], got[:, :, MID // 4 :].reshape(devices, room)
    every_view = early[:, :clips]
    every_alive = (every_view < videos_all).astype(f32)
    counts = jnp.sum(every_alive, axis=1, keepdims=True) * FRAME_ROWS
    start = clips + own_videos * classes
    every_cotangent = early[:, clips:start].reshape(videos_all, classes)
    params = []
    for vector in vectors:
        params.append(early[::rep_count, start : start + vector.shape[0]].reshape(1, -1))
        start += vector.shape[0]
    g_one, s_one, g_two, s_two, g_three, s_three = params
    video_count = jnp.sum(
        (every_view.reshape(1, -1) == video_list.astype(f32)[:, None]).astype(f32), axis=1
    )
    every_share = every_cotangent / video_count[:, None]
    own_place = lax.axis_index("fsdp") * rep_count + lax.axis_index("rep")
    own_counts = lax.dynamic_slice_in_dim(video_count, own_place * own_videos, own_videos)
    logit_grad = jnp.sum(members[:, :, None] * every_share[:, None, :], axis=0)
    logit_grad = jnp.pad(logit_grad.astype(bf16), ((0, 8 - clips), (0, 256 - classes)))
    stack_spatial = moves.across_again(*moves.across_both(*moves.stack(30, high)))
    norm_one, hidden, diff_even, diff_odd, summary = run(
        difference_kernel, "difference", 0.2,
        whole(got, counts, first, g_one, s_one, following, later),
        whole(shaped((2, MID)), in_grid, packed, packed, shaped((planes, MID))), [natural, field],
    )
    quad_diff = moves.complete(*stack_diff)
    wide = moves.along_z(run.hold(pieces[3]))
    gating, boost_even, boost_odd = run(
        gate_kernel, "gate", 0.2, [*whole(diff_even, diff_odd, summary, hidden), *quad_diff],
        whole(in_grid, packed, packed), [field, w_mid, w_small, dma(16), dma(16)],
    )
    quad_high = moves.complete_quarters(stack_spatial[0], *map(run.hold, stack_spatial[1:]))
    stack_wide = moves.across(*moves.stack(2, wide))
    second, note = run(
        spatial_kernel, "spatial", 13, [alive_in, *whole(boost_even, boost_odd), *quad_high],
        whole(shaped(tall), narrow_note), [natural, field, w_mid, dma(32)],
    )
    got = exchange(note)
    quad_wide = [(quad, WHOLE) for quad, _ in moves.complete(*stack_wide)]
    w_expand, w_class = run(
        wide_kernel, "wide", 2, quad_wide, whole(shaped((MID, D), bf16), shaped((D, 256), bf16))
    )
    norm_two, hidden_two, third, note = run(
        expand_kernel, "expand", 9,
        [alive_in, *whole(got, counts), *per_clip(second), *whole(g_two, s_two, w_expand)],
        [*whole(shaped((2, MID))), *per_clip(shaped(tall, bf16), shaped(tall_wide)), *whole(wide_note)],
        [pltpu.VMEM((clips, 1, D), f32)] * 2, clips,
    )
    got = exchange(note)
    part = shaped((8, 144, 256), bf16)
    norm_three, normed, summed_grad, note, video_sums, grad_class, class_theirs, class_mine = run(
        outcome_kernel, "outcome", 17,
        [
            alive_in, *whole(got, counts), *per_clip(third, clips_in),
            *whole(g_three, s_three, logit_grad, members, w_class),
        ],
        [
            *whole(shaped((2, D))), *per_clip(shaped(tall_wide, bf16), shaped(tall_wide, bf16)),
            *whole(wide_note, shaped((videos_all, 256)), shaped((D, 256), bf16), part, part),
        ],
        [
            pltpu.VMEM((8, D), f32), pltpu.VMEM((2, D), f32),
            pltpu.VMEM((8, D), f32), pltpu.VMEM((2, D), f32),
        ],
        clips,
    )
    got = exchange(note)
    expand_theirs, expand_mine, pre_two_grad, note, grads_three = run(
        third_kernel, "third", 18,
        [
            alive_in, *whole(got, counts), *per_clip(normed, summed_grad), *whole(g_three, norm_three),
            *per_clip(hidden_two, second), *whole(norm_two, g_two, s_two, w_expand),
        ],
        [
            *whole(shaped((MID, D // 2), bf16), shaped((MID, D // 2), bf16)), *per_clip(shaped(tall)),
            *whole(narrow_note, shaped((2, D))),
        ],
        [
            pltpu.VMEM((MID, D), f32), pltpu.VMEM((2, MID), f32),
            pltpu.VMEM((FRAME_ROWS, D), bf16), pltpu.VMEM((3, D), f32),
        ],
        clips,
    )
    got = exchange(note)
    from_core = lambda array: swap(array, CORE) if on_block else jnp.zeros_like(array)
    if on_block:
        half = shaped((4, 400, 256), bf16)
        expand_sent, expand_kept = run(
            expand_cut_kernel, "expand_cut", 3,
            whole(expand_mine, from_core(expand_theirs), class_mine, from_core(class_theirs)), whole(half, half),
        )
        expand_there = swap(expand_sent, Y)
    grads_two, low_even, low_odd, *spatial_theirs, offset = run(
        second_kernel, "second", 10,
        [alive_in, *whole(got, counts, pre_two_grad, second, norm_two, g_two, g_one, s_one, boost_even, boost_odd)],
        whole(
            shaped((2, MID)), packed, packed, *[shaped((3 * MID, MID // 2), bf16)] * 3, shaped((MID, MID))
        ),
        [natural, field],
    )
    spatial_there = [from_core(part) for part in spatial_theirs]
    if on_block:
        expand_group = moves.fold(expand_kept, expand_there)
    narrow = shaped((9 * MID, 128), bf16)
    spatial_sent, spatial_kept = run(
        own_spatial_kernel, "own_spatial", 9, whole(boost_even, boost_odd, low_even, offset, *spatial_there),
        whole(narrow, narrow), [pltpu.VMEM((MID, MID // 2), bf16)],
    )
    if on_block:
        spatial_there = swap(spatial_sent, X)
    hidden_grad, gate_even, gate_odd, pooled_theirs, pooled_mine, summary_grad = run(
        boost_back_kernel, "boost_back", 18,
        [*whole(low_even, low_odd, hidden, gating, summary), *quad_high, *quad_diff],
        whole(
            in_grid, packed, packed, shaped((MID, MID // 2), bf16), shaped((MID, MID // 2), bf16),
            shaped((planes, MID)),
        ),
        [field, w_mid, w_small, dma(32), dma(16)],
    )
    diff_theirs = run(
        their_diff_kernel, "their_diff", 8, whole(diff_even, diff_odd, gate_even, pooled_theirs),
        whole(*[shaped((taps * MID, MID // 2), bf16) for taps in (4, 4, 2)]),
    )
    diff_there = [from_core(part) for part in diff_theirs]
    if on_block:
        expand_group = [moves.totals(expand_group)]
        spatial_sent, spatial_kept = moves.by_y(spatial_kept, [spatial_there], 576)
        spatial_there = swap(spatial_sent, Y)
    narrow = shaped((10 * MID, 128), bf16)
    diff_sent, diff_kept = run(
        own_diff_kernel, "own_diff", 9, whole(diff_even, diff_odd, gate_even, pooled_mine, *diff_there),
        whole(narrow, narrow), [pltpu.VMEM((MID, MID // 2), bf16)],
    )
    if on_block:
        diff_there = swap(diff_sent, X)
    pre_one_grad, note = run(
        diff_back_kernel, "diff_back", 17,
        [
            alive_in, *whole(gate_even, gate_odd, summary_grad, hidden_grad, first, norm_one, g_one, s_one),
            *whole(before, earlier, later), *quad_diff,
        ],
        whole(shaped(tall), narrow_note), [natural, field, w_mid, dma(16)],
    )
    got = exchange(note)
    if on_block:
        spatial_group = moves.fold(spatial_kept, spatial_there)
        diff_sent, diff_kept = moves.by_y(diff_kept, [diff_there], 576, 64)
        diff_there = swap(diff_sent, Y)
    grads_one, low, *reduce_theirs, reduce_mine = run(
        reduce_kernel, "reduce", 9,
        [
            alive_in, *whole(got, counts), *per_clip(pre_one_grad, first), *whole(norm_one, g_one),
            *per_clip(clips_in),
        ],
        [
            *whole(shaped((2, MID))), *per_clip(shaped(tall, bf16)),
            *whole(*[shaped((D // 2, MID // 2), bf16)] * 2, shaped((D, MID // 2), bf16)),
        ],
        [pltpu.VMEM((D, MID), f32)], clips,
    )
    reduce_there = [from_core(part) for part in reduce_theirs]
    if on_block:
        spatial_group = [moves.totals(spatial_group)]
        diff_group = moves.fold(diff_kept, diff_there)
        reduce_sent, reduce_kept = moves.by_y(reduce_mine, reduce_there, 256)
        reduce_there = swap(reduce_sent, Y)
    (clips_grad,) = run(
        input_kernel, "input", 9, [*per_clip(low), *quad_reduce, *per_clip(summed_grad)],
        per_clip(shaped(tall_wide, bf16)), [pltpu.VMEM((D, MID), bf16), dma(16)], clips,
    )

    if on_block:
        run.factor = 6.0
        total = moves.totals(expand_group, diff_group, spatial_group)
        reduce_group = moves.fold(reduce_kept, reduce_there)
        (total,) = run(
            meet_kernel, "meet", 2, whole(total, swap(total, X)), whole(shaped((1616, 256), bf16))
        )
        total_there = swap(total, CORE)
        rest = moves.totals(reduce_group)
        rest_there = swap(rest, X)
        shapes = ((64, D), (256, classes), (1, classes), (576, MID), (64, MID), (576, MID))
        out_expand, out_class, video_logits, out_diff, out_pooled, out_spatial = run(
            finish_kernel, "finish", 3, whole(total, total_there, own_counts[:, None]),
            whole(*map(shaped, shapes)),
        )
        rest = moves.totals([rest, rest_there])
        (out_reduce,) = run(join_kernel, "join", 2, whole(rest, swap(rest, CORE)), whole(shaped((256, MID))))
    else:
        out_spatial = moves.scatter(moves.both_x(spatial_sent, spatial_kept), jnp.concatenate(spatial_theirs))
        out_expand = moves.scatter(expand_mine, expand_theirs)
        half, diff_theirs = moves.both_x(diff_sent, diff_kept), jnp.concatenate(diff_theirs)
        out_diff = moves.scatter(half[: 9 * MID], diff_theirs[: 9 * MID])
        out_pooled = moves.scatter(half[9 * MID :], diff_theirs[9 * MID :])
        out_reduce = moves.scatter(reduce_mine, jnp.concatenate(reduce_theirs))
        out_class = moves.scatter_rows(grad_class)[:, :classes]
        video_total = lax.psum_scatter(video_sums, EVERY, scatter_dimension=0, tiled=True)
        video_logits = video_total[:, :classes] / own_counts[:, None]
    def own_piece(grads, row):
        length = grads.shape[1] // fsdp_count
        return lax.dynamic_slice(grads, (row, lax.axis_index("fsdp") * length), (1, length))[0]

    return (
        video_logits,
        clips_grad,
        out_reduce,
        own_piece(grads_one, 1),
        own_piece(grads_one, 0),
        out_diff,
        out_pooled,
        out_spatial,
        own_piece(grads_two, 1),
        own_piece(grads_two, 0),
        out_expand,
        own_piece(grads_three, 1),
        own_piece(grads_three, 0),
        out_class,
    )


def solution(mesh):
    clips, weight, vector = P(EVERY, None, None), P("fsdp", None), P("fsdp")
    rows = P(EVERY, None)
    placed = (
        clips, P(EVERY), rows,
        weight, vector, vector,
        weight, weight, weight, vector, vector,
        weight, vector, vector,
        weight, rows,
    )
    return jax.shard_map(
        local,
        mesh=mesh,
        in_specs=placed,
        out_specs=(
            rows, clips,
            weight, vector, vector,
            weight, weight, weight, vector, vector,
            weight, vector, vector,
            weight,
        ),
        check_vma=False,
    )
```
